32 devices in a mesh: fib: 8 (over y, x, core), blk: 4 (over z).
Axes of the slice: x: 2, y: 2, z: 4, core: 2. Of those that a mesh axis runs over, the one named last changes fastest.
Arguments:
- field_data: float32 [33, 8, 512, 128], P(None, 'blk', 'fib'), may hold values from -120 to 120
- start_block: float32 [512, 64], replicated, may hold values from -6 to 6
Outputs:
- core_out: float32 [33, 8, 64, 128], P(None, 'blk', 'fib')
The draws below stay inside these ranges and needn't reach their ends.
All inputs are finite; a program needn't handle non-finite values.
Results may differ from the reference program's by a relative error of at most 0.00013.
Values sent between devices are 32-bit elements; how exact they have to be, the bound alone decides.
No kernel may reach another device: no remote copies, remote signals or barrier semaphores. Data moves between devices by JAX's collectives and lax.ppermute only.
A program may use at most 192 MiB of HBM per device.

```python
import jax
import jax.numpy as jnp
from jax import lax

S = 33
NX = 512
RANK = 64
NY = 128
NZ = 8


def draw_field_data(key, part):
    key_base = jax.random.fold_in(key, 11)
    key_species = jax.random.fold_in(key, 12)
    key_column = jax.random.fold_in(key, 13)
    key_plane = jax.random.fold_in(key, 14)
    shape_full = (S, NZ, NX, NY)
    base_values = jnp.clip(jax.random.normal(key_base, shape_full, jnp.float32), -5.0, 5.0)
    species_scale = jnp.exp(jax.random.uniform(key_species, (S, 1, 1, 1), jnp.float32, jnp.log(0.3), jnp.log(3.0)))
    column_scale = jnp.exp(jax.random.uniform(key_column, (1, 1, NX, 1), jnp.float32, 0.0, jnp.log(4.0)))
    plane_scale = jnp.exp(jax.random.uniform(key_plane, (1, NZ, 1, 1), jnp.float32, jnp.log(0.5), jnp.log(2.0)))
    return (base_values * species_scale * column_scale * plane_scale).astype(jnp.float32)


def noise(stream_key, shape, spread, limit, held_as=jnp.bfloat16):
    return jnp.clip(spread * jax.random.normal(stream_key, shape, jnp.float32), -limit, limit).astype(held_as)


def setup_inputs(seed: int = 0) -> dict:
    splits = jax.random.split(jax.random.key(seed), 3)
    field_data = draw_field_data(jax.random.fold_in(splits[2], 71), 0)
    start_block = noise(splits[1], (NX, RANK), 1.0, 6.0, jnp.float32)
    return {"field_data": field_data, "start_block": start_block}


def reference(field_data, start_block):
    highest = lax.Precision.HIGHEST

    def accumulate(running, slab_part):
        return (running + jnp.einsum('zxy,zwy->xw', slab_part, slab_part, precision=highest), None)
    gram_total, _ = lax.scan(accumulate, jnp.zeros((NX, NX), jnp.float32), field_data)
    raw_basis = jnp.dot(gram_total, start_block, precision=highest)
    inner_block = jnp.dot(raw_basis.T, raw_basis, precision=highest)
    lower_factor = jnp.linalg.cholesky(inner_block)
    basis_cols = jax.scipy.linalg.solve_triangular(lower_factor, raw_basis.T, lower=True).T
    core_out = jnp.einsum('szxy,xr->szry', field_data, basis_cols, precision=highest)
    return core_out
```

```python
import functools

import jax
import jax.numpy as jnp
from jax import lax
from jax.experimental import pallas as pl
from jax.experimental.pallas import tpu as pltpu
from jax.sharding import PartitionSpec as P

F32, BF16 = jnp.float32, jnp.bfloat16
HIGHEST = lax.Precision.HIGHEST
NN = (((1,), (0,)), ((), ()))
NT = (((1,), (1,)), ((), ()))
VMEM_LIMIT = 40 * 1024 * 1024
PARAMS = pltpu.CompilerParams(vmem_limit_bytes=VMEM_LIMIT)


def halves(value):
    high = value.astype(BF16)
    return high, (value - high.astype(F32)).astype(BF16)


def dot(left, right, dims):
    return lax.dot_general(left, right, dims, preferred_element_type=F32)


def dot_split(left, right, dims):
    rows = left.shape[0] // 2
    right_high, right_low = right
    both = dot(left, right_high, dims)
    return both[:rows] + both[rows:] + dot(left[:rows], right_low, dims)


def stack(value):
    return jnp.concatenate(halves(value), axis=0)


def pack_kernel(cells, slabs_ref, left_ref, send_ref, turned):
    own, width, ny = slabs_ref.shape
    left = left_ref.shape[0]
    g = pl.program_id(0)

    @pl.when(g == 0)
    def _():
        turned[:, : left * width] = left_ref[...].reshape(left * width, ny).T

    send_ref[0, : own * width] = slabs_ref[...].reshape(own * width, ny)
    send_ref[0, own * width :] = turned[pl.ds(pl.multiple_of(g * cells, cells), cells), :]


def pack(slabs, n, own, left):
    total, width, ny = slabs.shape
    cells = ny // n
    rows = own * width + cells
    return pl.pallas_call(
        functools.partial(pack_kernel, cells),
        grid=(n,),
        in_specs=[
            pl.BlockSpec((own, width, ny), lambda g: (g, 0, 0)),
            pl.BlockSpec((left, width, ny), lambda g: (n * own // left, 0, 0)),
        ],
        out_specs=pl.BlockSpec((1, rows, ny), lambda g: (g, 0, 0)),
        out_shape=jax.ShapeDtypeStruct((n, rows, ny), F32),
        scratch_shapes=[pltpu.VMEM((ny, ny), F32)],
        compiler_params=PARAMS,
    )(slabs, slabs)


def raw_kernel(left, width, slab_ref, rest_ref, start_ref, out_ref, start_two, total):
    n, _, ny = slab_ref.shape
    rank = start_ref.shape[0]
    s = pl.program_id(0)

    @pl.when(s == 0)
    def _():
        start_two[...] = stack(start_ref[...])
        cells = rest_ref.shape[1]
        columns = [halves(rest_ref[f]) for f in range(n)]
        for k in range(left):
            lanes = slice(k * width, (k + 1) * width)
            projected = jnp.zeros((rank, cells), F32)
            for f in range(n):
                part = [half[:, lanes] for half in columns[f]]
                projected += dot_split(start_two[:, f * width : (f + 1) * width], part, NT)
            two = stack(projected)
            for f in range(n):
                part = [half[:, lanes] for half in columns[f]]
                value = dot_split(two, part, NN)
                at = slice(f * width, (f + 1) * width)
                total[:, at] = value if k == 0 else total[:, at] + value

    block = halves(slab_ref[...].reshape(n * width, ny))
    projected = dot_split(start_two[...], block, NN)
    total[...] += dot_split(stack(projected), block, NT)

    @pl.when(s == pl.num_programs(0) - 1)
    def _():
        out_ref[...] = total[...]


def raw_basis(received, start_t, n, own, left, width):
    rows, ny = received.shape[1:]
    rank, nx = start_t.shape
    cells = rows - own * width
    return pl.pallas_call(
        functools.partial(raw_kernel, left, width),
        grid=(own,),
        in_specs=[
            pl.BlockSpec((n, width, ny), lambda s: (0, s, 0)),
            pl.BlockSpec((n, cells, ny), lambda s: (0, own * width // cells, 0)),
            pl.BlockSpec((rank, nx), lambda s: (0, 0)),
        ],
        out_specs=pl.BlockSpec((rank, nx), lambda s: (0, 0)),
        out_shape=jax.ShapeDtypeStruct((rank, nx), F32),
        scratch_shapes=[pltpu.VMEM((2 * rank, nx), BF16), pltpu.VMEM((rank, nx), F32)],
        compiler_params=PARAMS,
    )(received, received, start_t)


def inverse_factor(gram):
    rank = gram.shape[0]
    row = lax.broadcasted_iota(jnp.int32, (rank, rank), 0)
    col = lax.broadcasted_iota(jnp.int32, (rank, rank), 1)
    table = jnp.concatenate([gram, jnp.where(row == col, 1.0, 0.0).astype(F32)], axis=1)
    blocks = [table[8 * b : 8 * b + 8] for b in range(rank // 8)]
    sub = lax.broadcasted_iota(jnp.int32, (8, 1), 0)
    for j in range(rank):
        b, k = divmod(j, 8)
        pivot = blocks[b][k : k + 1]
        scaled = pivot * (1.0 / pivot[:, j : j + 1])
        for i in range(b, rank // 8):
            factor = blocks[i][:, j : j + 1]
            if i == b:
                factor = jnp.where(sub > k, factor, 0.0)
            blocks[i] = blocks[i] - factor * scaled
    table = jnp.concatenate(blocks, axis=0)
    diagonal = jnp.sum(jnp.where(row == col, table[:, :rank], 0.0), axis=1, keepdims=True)
    return table[:, rank:] * lax.rsqrt(diagonal)


def core_kernel(left, width, slab_ref, rest_ref, raw_ref, out_ref, basis_two):
    n, _, ny = slab_ref.shape
    rank = raw_ref.shape[0]
    each = rank // n
    s = pl.program_id(0)

    @pl.when(s == 0)
    def _():
        raw = raw_ref[...]
        gram = lax.dot_general(raw, raw, NT, precision=HIGHEST, preferred_element_type=F32)
        inverse = inverse_factor(gram)
        basis = lax.dot_general(inverse, raw, NN, precision=HIGHEST, preferred_element_type=F32)
        basis_two[...] = stack(basis)

    @pl.when(s < pl.num_programs(0) - 1)
    def _():
        block = halves(slab_ref[...].reshape(n * width, ny))
        out_ref[:, 0] = dot_split(basis_two[...], block, NN).reshape(n, each, ny)

    @pl.when(s == pl.num_programs(0) - 1)
    def _():
        cells = rest_ref.shape[1]
        columns = [halves(rest_ref[f]) for f in range(n)]
        out_ref[...] = jnp.zeros_like(out_ref)
        for k in range(left):
            lanes = slice(k * width, (k + 1) * width)
            value = jnp.zeros((rank, cells), F32)
            for f in range(n):
                part = [half[:, lanes] for half in columns[f]]
                value += dot_split(basis_two[:, f * width : (f + 1) * width], part, NT)
            out_ref[:, 0, :, k * cells : (k + 1) * cells] = value.reshape(n, each, cells)


def core(received, raw_t, n, own, left, width):
    rows, ny = received.shape[1:]
    rank, nx = raw_t.shape
    cells, each = rows - own * width, rank // n
    return pl.pallas_call(
        functools.partial(core_kernel, left, width),
        grid=(own + 1,),
        in_specs=[
            pl.BlockSpec((n, width, ny), lambda s: (0, jnp.minimum(s, own - 1), 0)),
            pl.BlockSpec((n, cells, ny), lambda s: (0, own * width // cells, 0)),
            pl.BlockSpec((rank, nx), lambda s: (0, 0)),
        ],
        out_specs=pl.BlockSpec((n, 1, each, ny), lambda s: (0, s, 0, 0)),
        out_shape=jax.ShapeDtypeStruct((n, own + 1, each, ny), F32),
        scratch_shapes=[pltpu.VMEM((2 * rank, nx), BF16)],
        compiler_params=PARAMS,
    )(received, received, raw_t)


def sum_over_devices(raw_t, devices):
    rank, nx = raw_t.shape
    tiles = (rank // 8) * (nx // 128)
    if tiles % devices:
        return lax.psum(raw_t, ("fib", "blk"))
    parts = raw_t.reshape(rank // 8, 8, nx // 128, 128).transpose(0, 2, 1, 3)
    parts = parts.reshape(devices, tiles // devices, 8, 128)
    terms = lax.all_to_all(parts, ("fib", "blk"), split_axis=0, concat_axis=0, tiled=True)
    mine = jnp.broadcast_to(jnp.sum(terms, axis=0, keepdims=True), terms.shape)
    whole = lax.all_to_all(mine, ("fib", "blk"), split_axis=0, concat_axis=0, tiled=True)
    return whole.reshape(rank // 8, nx // 128, 8, 128).transpose(0, 2, 1, 3).reshape(rank, nx)


def shards(n, devices, field_data, start_block):
    species, planes, width, ny = field_data.shape
    rank = start_block.shape[1]
    total = species * planes
    own, left = divmod(total, n)
    cells, each = ny // n, rank // n
    slabs = field_data.reshape(total, width, ny)
    send = pack(slabs, n, own, left)
    received = lax.all_to_all(send, "fib", split_axis=0, concat_axis=0, tiled=True)
    raw_t = sum_over_devices(raw_basis(received, start_block.T, n, own, left, width), devices)
    core_send = core(received, raw_t, n, own, left, width)
    core_got = lax.all_to_all(core_send, "fib", split_axis=0, concat_axis=0, tiled=True)
    out_main = core_got[:, :own].reshape(n * own, each, ny)
    out_rest = core_got[:, own, :, : left * cells].reshape(n, each, left, cells)
    out_rest = out_rest.transpose(2, 1, 0, 3).reshape(left, each, ny)
    return jnp.concatenate([out_main, out_rest], axis=0).reshape(species, planes, each, ny)


def solution(mesh):
    n, devices = mesh.shape["fib"], mesh.size
    in_specs = (P(None, "blk", "fib", None), P())
    out_specs = P(None, "blk", "fib", None)
    return jax.shard_map(
        functools.partial(shards, n, devices), mesh=mesh, in_specs=in_specs, out_specs=out_specs, check_vma=False
    )
```

```python
import functools

import jax
import jax.numpy as jnp
from jax import lax
from jax.experimental import pallas as pl
from jax.experimental.pallas import tpu as pltpu
from jax.sharding import PartitionSpec as P

F32, BF16 = jnp.float32, jnp.bfloat16
HIGHEST = lax.Precision.HIGHEST
NN = (((1,), (0,)), ((), ()))
NT = (((1,), (1,)), ((), ()))
VMEM_LIMIT = 40 * 1024 * 1024
PARAMS = pltpu.CompilerParams(vmem_limit_bytes=VMEM_LIMIT)


def halves(value):
    high = value.astype(BF16)
    return high, (value - high.astype(F32)).astype(BF16)


def dot(left, right, dims):
    return lax.dot_general(left, right, dims, preferred_element_type=F32)


def dot_split(left, right, dims):
    rows = left.shape[0] // 2
    right_high, right_low = right
    both = dot(left, right_high, dims)
    return both[:rows] + both[rows:] + dot(left[:rows], right_low, dims)


def stack(value):
    return jnp.concatenate(halves(value), axis=0)


def pack_kernel(cells, slabs_ref, left_ref, send_ref, turned):
    own, width, ny = slabs_ref.shape
    left = left_ref.shape[0]
    g = pl.program_id(0)

    @pl.when(g == 0)
    def _():
        turned[:, : left * width] = left_ref[...].reshape(left * width, ny).T

    send_ref[0, : own * width] = slabs_ref[...].reshape(own * width, ny)
    send_ref[0, own * width :] = turned[pl.ds(pl.multiple_of(g * cells, cells), cells), :]


def pack(slabs, n, own, left):
    total, width, ny = slabs.shape
    cells = ny // n
    rows = own * width + cells
    return pl.pallas_call(
        functools.partial(pack_kernel, cells),
        grid=(n,),
        in_specs=[
            pl.BlockSpec((own, width, ny), lambda g: (g, 0, 0)),
            pl.BlockSpec((left, width, ny), lambda g: (n * own // left, 0, 0)),
        ],
        out_specs=pl.BlockSpec((1, rows, ny), lambda g: (g, 0, 0)),
        out_shape=jax.ShapeDtypeStruct((n, rows, ny), F32),
        scratch_shapes=[pltpu.VMEM((ny, ny), F32)],
        compiler_params=PARAMS,
    )(slabs, slabs)


def by_cell(rest_ref, left, width):
    blocks = [rest_ref[f] for f in range(rest_ref.shape[0])]
    slabs = [[block[:, k * width : (k + 1) * width] for block in blocks] for k in range(left)]
    return jnp.concatenate([jnp.concatenate(parts, axis=1) for parts in slabs], axis=0)


def raw_kernel(own, left, width, cells_ref, start_ref, out_ref):
    n, _, ny = cells_ref.shape
    start = stack(start_ref[...])
    rest = halves(by_cell(cells_ref.at[:, own * width :], left, width))
    total = dot_split(stack(dot_split(start, rest, NT)), rest, NN)
    for s in range(own):
        slab = halves(cells_ref[:, s * width : (s + 1) * width].reshape(n * width, ny))
        total += dot_split(stack(dot_split(start, slab, NN)), slab, NT)
    out_ref[...] = total


def raw_basis(received, start_t, own, left, width):
    return pl.pallas_call(
        functools.partial(raw_kernel, own, left, width),
        in_specs=[pl.BlockSpec(memory_space=pltpu.VMEM)] * 2,
        out_specs=pl.BlockSpec(memory_space=pltpu.VMEM),
        out_shape=jax.ShapeDtypeStruct(start_t.shape, F32),
        compiler_params=PARAMS,
    )(received, start_t)


def inverse_factor(gram):
    rank = gram.shape[0]
    row = lax.broadcasted_iota(jnp.int32, (rank, rank), 0)
    col = lax.broadcasted_iota(jnp.int32, (rank, rank), 1)
    table = jnp.concatenate([gram, jnp.where(row == col, 1.0, 0.0).astype(F32)], axis=1)
    rows = [table[8 * b : 8 * b + 8] for b in range(rank // 8)]
    wide = rows[0].shape
    sub = lax.broadcasted_iota(jnp.int32, wide, 0)

    def spread(value, k):
        return jnp.broadcast_to(value[k : k + 1], wide)

    inverse = []
    for b in range(len(rows)):
        columns = [
            [jnp.broadcast_to(block[:, 8 * b + k : 8 * b + k + 1], wide) for k in range(8)] for block in rows[b:]
        ]
        pivots = jnp.ones(wide, F32)
        for k in range(8):
            pivot = spread(columns[0][k], k)
            pivots = jnp.where(sub == k, pivot, pivots)
            scale = 1.0 / pivot
            scaled = spread(rows[b], k) * scale
            ahead = [spread(columns[0][m], k) * scale for m in range(k + 1, 8)]
            for i, column in enumerate(columns):
                factor = jnp.where(sub > k, column[k], 0.0) if i == 0 else column[k]
                for m in range(k + 1, 8):
                    column[m] = column[m] - factor * ahead[m - k - 1]
                rows[b + i] = rows[b + i] - factor * scaled
        inverse.append(rows[b][:, rank:] * lax.rsqrt(pivots[:, rank:]))
    return jnp.concatenate(inverse, axis=0)


def core_kernel(own, left, width, cells_ref, raw_ref, out_ref):
    n, rows, ny = cells_ref.shape
    cells = rows - own * width
    rank = raw_ref.shape[0]
    each = rank // n
    raw = raw_ref[...]
    gram = lax.dot_general(raw, raw, NT, precision=HIGHEST, preferred_element_type=F32)
    basis = lax.dot_general(inverse_factor(gram), raw, NN, precision=HIGHEST, preferred_element_type=F32)
    basis = stack(basis)
    for s in range(own):
        slab = halves(cells_ref[:, s * width : (s + 1) * width].reshape(n * width, ny))
        out_ref[:, s] = dot_split(basis, slab, NN).reshape(n, each, ny)
    rest = halves(by_cell(cells_ref.at[:, own * width :], left, width))
    value = dot_split(basis, rest, NT)
    value = jnp.concatenate([value, jnp.zeros((rank, ny - left * cells), F32)], axis=1)
    out_ref[:, own] = value.reshape(n, each, ny)


def core(received, raw_t, own, left, width):
    n, _, ny = received.shape
    return pl.pallas_call(
        functools.partial(core_kernel, own, left, width),
        in_specs=[pl.BlockSpec(memory_space=pltpu.VMEM)] * 2,
        out_specs=pl.BlockSpec(memory_space=pltpu.VMEM),
        out_shape=jax.ShapeDtypeStruct((n, own + 1, raw_t.shape[0] // n, ny), F32),
        compiler_params=PARAMS,
    )(received, raw_t)


def sum_over_devices(raw_t, devices):
    rank, nx = raw_t.shape
    tiles = (rank // 8) * (nx // 128)
    if tiles % devices:
        return lax.psum(raw_t, ("fib", "blk"))
    parts = raw_t.reshape(rank // 8, 8, nx // 128, 128).transpose(0, 2, 1, 3)
    parts = parts.reshape(devices, tiles // devices, 8, 128)
    terms = lax.all_to_all(parts, ("fib", "blk"), split_axis=0, concat_axis=0, tiled=True)
    mine = jnp.broadcast_to(jnp.sum(terms, axis=0, keepdims=True), terms.shape)
    whole = lax.all_to_all(mine, ("fib", "blk"), split_axis=0, concat_axis=0, tiled=True)
    return whole.reshape(rank // 8, nx // 128, 8, 128).transpose(0, 2, 1, 3).reshape(rank, nx)


def shards(n, devices, field_data, start_block):
    species, planes, width, ny = field_data.shape
    rank = start_block.shape[1]
    total = species * planes
    own, left = divmod(total, n)
    cells, each = ny // n, rank // n
    slabs = field_data.reshape(total, width, ny)
    send = pack(slabs, n, own, left)
    received = lax.all_to_all(send, "fib", split_axis=0, concat_axis=0, tiled=True)
    raw_t = sum_over_devices(raw_basis(received, start_block.T, own, left, width), devices)
    core_send = core(received, raw_t, own, left, width)
    core_got = lax.all_to_all(core_send, "fib", split_axis=0, concat_axis=0, tiled=True)
    out_main = core_got[:, :own].reshape(n * own, each, ny)
    out_rest = core_got[:, own, :, : left * cells].reshape(n, each, left, cells)
    out_rest = out_rest.transpose(2, 1, 0, 3).reshape(left, each, ny)
    return jnp.concatenate([out_main, out_rest], axis=0).reshape(species, planes, each, ny)


def solution(mesh):
    n, devices = mesh.shape["fib"], mesh.size
    in_specs = (P(None, "blk", "fib", None), P())
    out_specs = P(None, "blk", "fib", None)
    return jax.shard_map(
        functools.partial(shards, n, devices), mesh=mesh, in_specs=in_specs, out_specs=out_specs, check_vma=False
    )
```

```python
import functools

import jax
import jax.numpy as jnp
from jax import lax
from jax.experimental import pallas as pl
from jax.experimental.pallas import tpu as pltpu
from jax.sharding import PartitionSpec as P

F32, BF16 = jnp.float32, jnp.bfloat16
HIGHEST = lax.Precision.HIGHEST
NN = (((1,), (0,)), ((), ()))
NT = (((1,), (1,)), ((), ()))
VMEM_LIMIT = 40 * 1024 * 1024
PARAMS = pltpu.CompilerParams(vmem_limit_bytes=VMEM_LIMIT)


def halves(value):
    high = value.astype(BF16)
    return high, (value - high.astype(F32)).astype(BF16)


def dot(left, right, dims):
    return lax.dot_general(left, right, dims, preferred_element_type=F32)


def dot_split(left, right, dims):
    rows = left.shape[0] // 2
    right_high, right_low = right
    both = dot(left, right_high, dims)
    return both[:rows] + both[rows:] + dot(left[:rows], right_low, dims)


def stack(value):
    return jnp.concatenate(halves(value), axis=0)


def partners(n):
    return [[(i, i ^ k) for i in range(n)] for k in range(1, n)]


def reorder(value, me, n):
    width = value.shape[1] // n
    bit = 1
    while bit < n:
        step = bit * width
        parts = [value[:, i * step : (i + 1) * step] for i in range(n // bit)]
        swapped = jnp.concatenate([parts[i ^ 1] for i in range(n // bit)], axis=1)
        value = jnp.where((me & bit) != 0, swapped, value)
        bit *= 2
    return value


def pack_kernel(n, own, left, width, me_ref, rows_ref, *refs):
    blocks, (turned, rest, sems) = refs[:n], refs[n:]
    ny = rows_ref.shape[1]
    cells = ny // n
    me = me_ref[0]
    first = pltpu.make_async_copy(rows_ref.at[pl.ds(n * own * width, left * width)], rest, sems.at[n])
    first.start()
    copies = []
    for k, block in enumerate(blocks):
        source = rows_ref.at[pl.ds((me ^ k) * (own * width), own * width)]
        copies.append(pltpu.make_async_copy(source, block.at[pl.ds(0, own * width)], sems.at[k]))
        copies[-1].start()
    first.wait()
    turned[:, : left * width] = rest[...].T
    for k, block in enumerate(blocks):
        at = pl.multiple_of((me ^ k) * cells, cells)
        block[own * width :] = turned[pl.ds(at, cells), :]
    for copy in copies:
        copy.wait()


def pack(rows, me, n, own, left, width):
    ny = rows.shape[1]
    return pl.pallas_call(
        functools.partial(pack_kernel, n, own, left, width),
        in_specs=[pl.BlockSpec(memory_space=pltpu.SMEM), pl.BlockSpec(memory_space=pltpu.HBM)],
        out_specs=[pl.BlockSpec(memory_space=pltpu.VMEM)] * n,
        out_shape=[jax.ShapeDtypeStruct((own * width + ny // n, ny), F32)] * n,
        scratch_shapes=[
            pltpu.VMEM((ny, ny), F32),
            pltpu.VMEM((left * width, ny), F32),
            pltpu.SemaphoreType.DMA((n + 1,)),
        ],
        compiler_params=PARAMS,
    )(me, rows)


def by_cell(refs, own, left, width):
    blocks = [ref[own * width :] for ref in refs]
    slabs = [[block[:, k * width : (k + 1) * width] for block in blocks] for k in range(left)]
    return jnp.concatenate([jnp.concatenate(parts, axis=1) for parts in slabs], axis=0)


def slab_of(refs, s, width):
    return halves(jnp.concatenate([ref[s * width : (s + 1) * width] for ref in refs], axis=0))


def raw_kernel(own, left, width, me_ref, start_ref, *refs):
    refs, out_ref = refs[:-1], refs[-1]
    n, me = len(refs), me_ref[0]
    start = stack(reorder(start_ref[...], me, n))
    rest = halves(by_cell(refs, own, left, width))
    total = dot_split(stack(dot_split(start, rest, NT)), rest, NN)
    for s in range(own):
        slab = slab_of(refs, s, width)
        total += dot_split(stack(dot_split(start, slab, NN)), slab, NT)
    out_ref[...] = reorder(total, me, n)


def raw_basis(blocks, start_t, me, own, left, width):
    specs = [pl.BlockSpec(memory_space=pltpu.SMEM)] + [pl.BlockSpec(memory_space=pltpu.VMEM)] * (len(blocks) + 1)
    return pl.pallas_call(
        functools.partial(raw_kernel, own, left, width),
        in_specs=specs,
        out_specs=pl.BlockSpec(memory_space=pltpu.VMEM),
        out_shape=jax.ShapeDtypeStruct(start_t.shape, F32),
        compiler_params=PARAMS,
    )(me, start_t, *blocks)


def inverse_factor(gram):
    rank = gram.shape[0]
    row = lax.broadcasted_iota(jnp.int32, (rank, rank), 0)
    col = lax.broadcasted_iota(jnp.int32, (rank, rank), 1)
    table = jnp.concatenate([gram, jnp.where(row == col, 1.0, 0.0).astype(F32)], axis=1)
    rows = [table[8 * b : 8 * b + 8] for b in range(rank // 8)]
    wide = rows[0].shape
    sub = lax.broadcasted_iota(jnp.int32, wide, 0)

    def spread(value, k):
        return jnp.broadcast_to(value[k : k + 1], wide)

    inverse = []
    for b in range(len(rows)):
        columns = [
            [jnp.broadcast_to(block[:, 8 * b + k : 8 * b + k + 1], wide) for k in range(8)] for block in rows[b:]
        ]
        pivots = jnp.ones(wide, F32)
        for k in range(8):
            pivot = spread(columns[0][k], k)
            pivots = jnp.where(sub == k, pivot, pivots)
            scale = 1.0 / pivot
            scaled = spread(rows[b], k) * scale
            ahead = [spread(columns[0][m], k) * scale for m in range(k + 1, 8)]
            for i, column in enumerate(columns):
                factor = jnp.where(sub > k, column[k], 0.0) if i == 0 else column[k]
                for m in range(k + 1, 8):
                    column[m] = column[m] - factor * ahead[m - k - 1]
                rows[b + i] = rows[b + i] - factor * scaled
        inverse.append(rows[b][:, rank:] * lax.rsqrt(pivots[:, rank:]))
    return jnp.concatenate(inverse, axis=0)


def core_kernel(own, left, width, me_ref, raw_ref, *refs):
    refs, out_ref = refs[:-1], refs[-1]
    n, ny = len(refs), out_ref.shape[-1]
    rank = raw_ref.shape[0]
    each = rank // n
    raw = reorder(raw_ref[...], me_ref[0], n)
    gram = lax.dot_general(raw, raw, NT, precision=HIGHEST, preferred_element_type=F32)
    basis = lax.dot_general(inverse_factor(gram), raw, NN, precision=HIGHEST, preferred_element_type=F32)
    basis = stack(basis)
    for s in range(own):
        out_ref[:, s] = dot_split(basis, slab_of(refs, s, width), NN).reshape(n, each, ny)
    value = dot_split(basis, halves(by_cell(refs, own, left, width)), NT)
    value = jnp.concatenate([value, jnp.zeros((rank, ny - value.shape[1]), F32)], axis=1)
    out_ref[:, own] = value.reshape(n, each, ny)


def core(blocks, raw_t, me, own, left, width):
    n, ny = len(blocks), blocks[0].shape[-1]
    return pl.pallas_call(
        functools.partial(core_kernel, own, left, width),
        in_specs=[pl.BlockSpec(memory_space=pltpu.SMEM)] + [pl.BlockSpec(memory_space=pltpu.VMEM)] * (n + 1),
        out_specs=pl.BlockSpec(memory_space=pltpu.VMEM),
        out_shape=jax.ShapeDtypeStruct((n, own + 1, raw_t.shape[0] // n, ny), F32),
        compiler_params=PARAMS,
    )(me, raw_t, *blocks)


def sum_over_devices(raw_t, devices):
    rank, nx = raw_t.shape
    tiles = (rank // 8) * (nx // 128)
    if tiles % devices:
        return lax.psum(raw_t, ("fib", "blk"))
    parts = raw_t.reshape(rank // 8, 8, nx // 128, 128).transpose(0, 2, 1, 3)
    parts = parts.reshape(devices, tiles // devices, 8, 128)
    terms = lax.all_to_all(parts, ("fib", "blk"), split_axis=0, concat_axis=0, tiled=True)
    mine = jnp.broadcast_to(jnp.sum(terms, axis=0, keepdims=True), terms.shape)
    whole = lax.all_to_all(mine, ("fib", "blk"), split_axis=0, concat_axis=0, tiled=True)
    return whole.reshape(rank // 8, nx // 128, 8, 128).transpose(0, 2, 1, 3).reshape(rank, nx)


def shards(n, devices, field_data, start_block):
    species, planes, width, ny = field_data.shape
    rank = start_block.shape[1]
    total = species * planes
    own, left = divmod(total, n)
    cells, each = ny // n, rank // n
    me = lax.axis_index("fib").astype(jnp.int32).reshape(1)
    blocks = pack(field_data.reshape(total * width, ny), me, n, own, left, width)
    got = [lax.ppermute(block, "fib", pairs) for block, pairs in zip(blocks[1:], partners(n))]
    blocks = [blocks[0], *got]
    raw_t = sum_over_devices(raw_basis(blocks, start_block.T, me, own, left, width), devices)
    core_send = core(blocks, raw_t, me, own, left, width)
    core_got = lax.all_to_all(core_send, "fib", split_axis=0, concat_axis=0, tiled=True)
    out_main = core_got[:, :own].reshape(n * own, each, ny)
    out_rest = core_got[:, own, :, : left * cells].reshape(n, each, left, cells)
    out_rest = out_rest.transpose(2, 1, 0, 3).reshape(left, each, ny)
    return jnp.concatenate([out_main, out_rest], axis=0).reshape(species, planes, each, ny)


def solution(mesh):
    n, devices = mesh.shape["fib"], mesh.size
    in_specs = (P(None, "blk", "fib", None), P())
    out_specs = P(None, "blk", "fib", None)
    return jax.shard_map(
        functools.partial(shards, n, devices), mesh=mesh, in_specs=in_specs, out_specs=out_specs, check_vma=False
    )
```

```python
import functools

import jax
import jax.numpy as jnp
from jax import lax
from jax.experimental import pallas as pl
from jax.experimental.pallas import tpu as pltpu
from jax.sharding import PartitionSpec as P

F32, BF16 = jnp.float32, jnp.bfloat16
HIGHEST = lax.Precision.HIGHEST
NN = (((1,), (0,)), ((), ()))
NT = (((1,), (1,)), ((), ()))
PARAMS = pltpu.CompilerParams(vmem_limit_bytes=40 * 1024 * 1024)
VMEM = pl.BlockSpec(memory_space=pltpu.VMEM)
SMEM = pl.BlockSpec(memory_space=pltpu.SMEM)
HBM = pl.BlockSpec(memory_space=pltpu.HBM)


def halves(value):
    high = value.astype(BF16)
    return high, (value - high.astype(F32)).astype(BF16)


def stack(value):
    return jnp.concatenate(halves(value), axis=0)


def dot(left, right, dims):
    return lax.dot_general(left, right, dims, preferred_element_type=F32)


def dot_split(left, right, dims):
    rows = left.shape[0] // 2
    right_high, right_low = right
    both = dot(left, right_high, dims)
    return both[:rows] + both[rows:] + dot(left[:rows], right_low, dims)


def reorder(value, me, n, axis):
    width = value.shape[axis] // n
    bit = 1
    while bit < n:
        parts = [lax.slice_in_dim(value, i * bit * width, (i + 1) * bit * width, axis=axis) for i in range(n // bit)]
        swapped = jnp.concatenate([parts[i ^ 1] for i in range(n // bit)], axis=axis)
        value = jnp.where((me & bit) != 0, swapped, value)
        bit *= 2
    return value


def exchange(value, axis, mask, size):
    return lax.ppermute(value, axis, [(i, i ^ mask) for i in range(size)])


def pack_kernel(chips, first, last, own, left, width, me_ref, rows_ref, *refs):
    blocks, refs = refs[:chips], refs[chips:]
    ny = rows_ref.shape[1]
    chip = lax.div(me_ref[0], 2)
    sems = refs[-1]
    count = (last - first) * width
    if left:
        turned, rest = refs[:2]
        rest_copy = pltpu.make_async_copy(rows_ref.at[pl.ds(chips * own * width, left * width)], rest, sems.at[chips])
        rest_copy.start()
    copies = []
    for k, block in enumerate(blocks):
        at = pl.multiple_of(((chip ^ k) * own + first) * width, 8)
        copies.append(pltpu.make_async_copy(rows_ref.at[pl.ds(at, count)], block.at[pl.ds(0, count)], sems.at[k]))
        copies[-1].start()
    if left:
        cells = ny // chips
        rest_copy.wait()
        turned[:, : left * width] = rest[...].T
        for k, block in enumerate(blocks):
            block[count:] = turned[pl.ds(pl.multiple_of((chip ^ k) * cells, cells), cells), :]
    for copy in copies:
        copy.wait()


def pack(rows, me, chips, first, last, own, left, width):
    ny = rows.shape[1]
    high = (last - first) * width + (ny // chips if left else 0)
    scratch = [pltpu.VMEM((ny, ny), F32), pltpu.VMEM((left * width, ny), F32)] if left else []
    return pl.pallas_call(
        functools.partial(pack_kernel, chips, first, last, own, left, width),
        in_specs=[SMEM, HBM],
        out_specs=[VMEM] * chips,
        out_shape=[jax.ShapeDtypeStruct((high, ny), F32)] * chips,
        scratch_shapes=scratch + [pltpu.SemaphoreType.DMA((chips + 1,))],
        compiler_params=PARAMS,
    )(me, rows)


def slabs_of(refs, count, width):
    ny = refs[0].shape[1]
    for s in range(0, count, 2):
        pair = range(s, min(s + 2, count))
        columns = [jnp.concatenate([ref[q * width : (q + 1) * width] for ref in refs], axis=0) for q in pair]
        yield s * ny, (s + len(columns)) * ny, halves(jnp.concatenate(columns, axis=1))


def rest_of(refs, count, left, width):
    blocks = [ref[count * width :] for ref in refs]
    slabs = [[block[:, k * width : (k + 1) * width] for block in blocks] for k in range(left)]
    return halves(jnp.concatenate([jnp.concatenate(parts, axis=1) for parts in slabs], axis=0))


def widen(value, lanes):
    return jnp.concatenate([value, jnp.zeros((value.shape[0], lanes - value.shape[1]), F32)], axis=1)


def project_kernel(count, left, width, me_ref, start_ref, *refs):
    refs, out_ref = refs[:-1], refs[-1]
    chips, me, ny = len(refs), me_ref[0], refs[0].shape[1]
    parts = [start_ref[:, i * width : (i + 1) * width] for i in range(2 * chips)]
    odd = (me & 1) != 0
    start = jnp.where(odd, jnp.concatenate(parts[1::2], axis=1), jnp.concatenate(parts[::2], axis=1))
    start = stack(reorder(start, lax.div(me, 2), chips, 1))
    for at, to, slab in slabs_of(refs, count, width):
        out_ref[:, at:to] = dot_split(start, slab, NN)
    if left:
        out_ref[:, count * ny :] = widen(dot_split(start, rest_of(refs, count, left, width), NT), ny)


def project(blocks, start_t, me, count, left, width):
    ny = blocks[0].shape[1]
    return pl.pallas_call(
        functools.partial(project_kernel, count, left, width),
        in_specs=[SMEM] + [VMEM] * (1 + len(blocks)),
        out_specs=VMEM,
        out_shape=jax.ShapeDtypeStruct((start_t.shape[0], (count + (left > 0)) * ny), F32),
        compiler_params=PARAMS,
    )(me, start_t, *blocks)


def raw_kernel(count, left, width, more, last, me_ref, mine_ref, other_ref, *refs):
    refs, out_ref = refs[:-1], refs[-1]
    if more:
        refs, total = refs[:-1], refs[-1][...]
    else:
        total = jnp.zeros(out_ref.shape, F32)
    ny = refs[0].shape[1]
    for at, to, slab in slabs_of(refs, count, width):
        total += dot_split(stack(mine_ref[:, at:to] + other_ref[:, at:to]), slab, NT)
    if left:
        rest = rest_of(refs, count, left, width)
        lanes = slice(count * ny, count * ny + rest[0].shape[0])
        total += dot_split(stack(mine_ref[:, lanes] + other_ref[:, lanes]), rest, NN)
    if last:
        total = reorder(total, lax.div(me_ref[0], 2), len(refs), 1)
    out_ref[...] = total


def raw_part(blocks, mine, other, before, me, count, left, width, last):
    more = [] if before is None else [before]
    return pl.pallas_call(
        functools.partial(raw_kernel, count, left, width, bool(more), last),
        in_specs=[SMEM] + [VMEM] * (2 + len(blocks) + len(more)),
        out_specs=VMEM,
        out_shape=jax.ShapeDtypeStruct((mine.shape[0], len(blocks) * width), F32),
        compiler_params=PARAMS,
    )(me, mine, other, *blocks, *more)


def sum_over(value, axis, low, size):
    while low < size:
        masks = [low] if 2 * low >= size else [low, 2 * low, 3 * low]
        got = [exchange(value, axis, mask, size) for mask in masks]
        for term in got:
            value = value + term
        low *= len(masks) + 1
    return value


def gram_kernel(raw_ref, out_ref):
    raw = raw_ref[...]
    out_ref[...] = lax.dot_general(raw, raw, NT, precision=HIGHEST, preferred_element_type=F32)


def gram_part(raw):
    return pl.pallas_call(
        gram_kernel,
        in_specs=[VMEM],
        out_specs=VMEM,
        out_shape=jax.ShapeDtypeStruct((raw.shape[0], raw.shape[0]), F32),
        compiler_params=PARAMS,
    )(raw)


def inverse_factor(gram):
    rank = gram.shape[0]
    row = lax.broadcasted_iota(jnp.int32, (rank, rank), 0)
    col = lax.broadcasted_iota(jnp.int32, (rank, rank), 1)
    table = jnp.concatenate([gram, jnp.where(row == col, 1.0, 0.0).astype(F32)], axis=1)
    rows = [table[8 * b : 8 * b + 8] for b in range(rank // 8)]
    wide = rows[0].shape
    sub = lax.broadcasted_iota(jnp.int32, wide, 0)

    def spread(value, k):
        return jnp.broadcast_to(value[k : k + 1], wide)

    inverse = []
    for b in range(len(rows)):
        columns = [
            [jnp.broadcast_to(block[:, 8 * b + k : 8 * b + k + 1], wide) for k in range(8)] for block in rows[b:]
        ]
        pivots = jnp.ones(wide, F32)
        for k in range(8):
            pivot = spread(columns[0][k], k)
            pivots = jnp.where(sub == k, pivot, pivots)
            scale = 1.0 / pivot
            scaled = spread(rows[b], k) * scale
            ahead = [spread(columns[0][m], k) * scale for m in range(k + 1, 8)]
            for i, column in enumerate(columns):
                factor = jnp.where(sub > k, column[k], 0.0) if i == 0 else column[k]
                for m in range(k + 1, 8):
                    column[m] = column[m] - factor * ahead[m - k - 1]
                rows[b + i] = rows[b + i] - factor * scaled
        inverse.append(rows[b][:, rank:] * lax.rsqrt(pivots[:, rank:]))
    return jnp.concatenate(inverse, axis=0)


def core_kernel(counts, left, width, me_ref, mine_ref, other_ref, raw_ref, *refs):
    refs, (keep_ref, send_ref) = refs[:-2], refs[-2:]
    chips = keep_ref.shape[0]
    rank, (each, ny) = raw_ref.shape[0], keep_ref.shape[-2:]
    me = me_ref[0]
    inverse = inverse_factor(mine_ref[...] + other_ref[...])
    inverse = reorder(inverse, me, 2 * chips, 0)
    raw = reorder(raw_ref[...], lax.div(me, 2), chips, 1)
    basis = stack(lax.dot_general(inverse, raw, NN, precision=HIGHEST, preferred_element_type=F32))

    def put(slab, value):
        for k in range(chips):
            keep_ref[k, slab] = value[2 * k * each : (2 * k + 1) * each]
            send_ref[k, slab] = value[(2 * k + 1) * each : (2 * k + 2) * each]

    done = 0
    for c, count in enumerate(counts):
        blocks = refs[c * chips : (c + 1) * chips]
        for at, to, slab in slabs_of(blocks, count, width):
            value = dot_split(basis, slab, NN)
            for lane in range(0, to - at, ny):
                put(done + (at + lane) // ny, value[:, lane : lane + ny])
        done += count
    put(done, widen(dot_split(basis, rest_of(blocks, count, left, width), NT), ny))


def core(blocks, mine, other, raw, me, counts, left, width, each):
    chips, ny = len(blocks) // len(counts), blocks[0].shape[1]
    shape = jax.ShapeDtypeStruct((chips, sum(counts) + 1, each, ny), F32)
    return pl.pallas_call(
        functools.partial(core_kernel, counts, left, width),
        in_specs=[SMEM] + [VMEM] * (3 + len(blocks)),
        out_specs=[VMEM] * 2,
        out_shape=[shape] * 2,
        compiler_params=PARAMS,
    )(me, mine, other, raw, *blocks)


def add_kernel(keep_ref, got_ref, *outs):
    for k, out in enumerate(outs):
        out[...] = keep_ref[k] + got_ref[k]


def add_parts(keep, got):
    chips = keep.shape[0]
    return pl.pallas_call(
        add_kernel,
        in_specs=[VMEM] * 2,
        out_specs=[VMEM] * chips,
        out_shape=[jax.ShapeDtypeStruct(keep.shape[1:], F32)] * chips,
        compiler_params=PARAMS,
    )(keep, got)


def place_kernel(own, left, cells, me_ref, *refs):
    refs, (out_ref, rest, sems) = refs[:-3], refs[-3:]
    chips = len(refs)
    chip = lax.div(me_ref[0], 2)
    copies = []
    for k, ref in enumerate(refs):
        to = out_ref.at[pl.ds((chip ^ k) * own, own)]
        copies.append(pltpu.make_async_copy(ref.at[pl.ds(0, own)], to, sems.at[k]))
        copies[-1].start()
    for k in range(left):
        parts = [ref[own][:, k * cells : (k + 1) * cells] for ref in refs]
        rest[k] = reorder(jnp.concatenate(parts, axis=1), chip, chips, 1)
    copies.append(pltpu.make_async_copy(rest, out_ref.at[pl.ds(chips * own, left)], sems.at[chips]))
    copies[-1].start()
    for copy in copies:
        copy.wait()


def place(parts, me, own, left):
    chips = len(parts)
    _, each, ny = parts[0].shape
    return pl.pallas_call(
        functools.partial(place_kernel, own, left, ny // chips),
        in_specs=[SMEM] + [VMEM] * chips,
        out_specs=HBM,
        out_shape=jax.ShapeDtypeStruct((chips * own + left, each, ny), F32),
        scratch_shapes=[pltpu.VMEM((left, each, ny), F32), pltpu.SemaphoreType.DMA((chips + 1,))],
        compiler_params=PARAMS,
    )(me, *parts)


def shards(n, layers, field_data, start_block):
    species, planes, width, ny = field_data.shape
    chips, each = n // 2, start_block.shape[1] // n
    total = species * planes
    own, left = divmod(total, chips)
    counts = [own - own // 2, own // 2]
    me = lax.axis_index("fib").astype(jnp.int32).reshape(1)
    rows = field_data.reshape(total * width, ny)
    start_t = start_block.T
    blocks, raw, first = [], None, 0
    for c, count in enumerate(counts):
        rest = left if c == len(counts) - 1 else 0
        sent = pack(rows, me, chips, first, first + count, own, rest, width)
        part = [sent[0]] + [exchange(sent[k], "fib", 2 * k, n) for k in range(1, chips)]
        mine = project(part, start_t, me, count, rest, width)
        other = exchange(mine, "fib", 1, n)
        raw = raw_part(part, mine, other, raw, me, count, rest, width, c == len(counts) - 1)
        blocks += part
        first += count
    raw = sum_over(sum_over(raw, "fib", 2, n), "blk", 1, layers)
    gram = gram_part(raw)
    keep, send = core(blocks, gram, exchange(gram, "fib", 1, n), raw, me, counts, left, width, each)
    parts = add_parts(keep, exchange(send, "fib", 1, n))
    parts = [parts[0]] + [exchange(parts[k], "fib", 2 * k, n) for k in range(1, chips)]
    return place(parts, me, own, left).reshape(species, planes, each, ny)


def solution(mesh):
    n, layers = mesh.shape["fib"], mesh.shape["blk"]
    in_specs = (P(None, "blk", "fib", None), P())
    out_specs = P(None, "blk", "fib", None)
    return jax.shard_map(
        functools.partial(shards, n, layers), mesh=mesh, in_specs=in_specs, out_specs=out_specs, check_vma=False
    )
```

```python
import functools

import jax
import jax.numpy as jnp
from jax import lax
from jax.experimental import pallas as pl
from jax.experimental.pallas import tpu as pltpu
from jax.sharding import PartitionSpec as P

F32, BF16 = jnp.float32, jnp.bfloat16
HIGHEST = lax.Precision.HIGHEST
NN = (((1,), (0,)), ((), ()))
NT = (((1,), (1,)), ((), ()))
PARAMS = pltpu.CompilerParams(vmem_limit_bytes=40 * 1024 * 1024)
VMEM = pl.BlockSpec(memory_space=pltpu.VMEM)
SMEM = pl.BlockSpec(memory_space=pltpu.SMEM)
HBM = pl.BlockSpec(memory_space=pltpu.HBM)


def halves(value):
    high = value.astype(BF16)
    return high, (value - high.astype(F32)).astype(BF16)


def stack(value):
    return jnp.concatenate(halves(value), axis=0)


def dot(left, right, dims):
    return lax.dot_general(left, right, dims, preferred_element_type=F32)


def dot_split(left, right, dims):
    rows = left.shape[0] // 2
    right_high, right_low = right
    both = dot(left, right_high, dims)
    return both[:rows] + both[rows:] + dot(left[:rows], right_low, dims)


def reorder(value, me, n, axis):
    width = value.shape[axis] // n
    bit = 1
    while bit < n:
        parts = [lax.slice_in_dim(value, i * bit * width, (i + 1) * bit * width, axis=axis) for i in range(n // bit)]
        swapped = jnp.concatenate([parts[i ^ 1] for i in range(n // bit)], axis=axis)
        value = jnp.where((me & bit) != 0, swapped, value)
        bit *= 2
    return value


def exchange(value, axis, mask, size):
    return lax.ppermute(value, axis, [(i, i ^ mask) for i in range(size)])


def pack_kernel(chips, first, last, own, left, width, me_ref, rows_ref, after, *refs):
    del after
    blocks, refs = refs[:chips], refs[chips:]
    ny = rows_ref.shape[1]
    chip = lax.div(me_ref[0], 2)
    sems = refs[-1]
    count = (last - first) * width
    if left:
        turned, rest = refs[:2]
        rest_copy = pltpu.make_async_copy(rows_ref.at[pl.ds(chips * own * width, left * width)], rest, sems.at[chips])
        rest_copy.start()
    copies = []
    for k, block in enumerate(blocks):
        at = pl.multiple_of(((chip ^ k) * own + first) * width, 8)
        copies.append(pltpu.make_async_copy(rows_ref.at[pl.ds(at, count)], block.at[pl.ds(0, count)], sems.at[k]))
        copies[-1].start()
    if left:
        cells = ny // chips
        rest_copy.wait()
        turned[:, : left * width] = rest[...].T
        for k, block in enumerate(blocks):
            block[count:] = turned[pl.ds(pl.multiple_of((chip ^ k) * cells, cells), cells), :]
    for copy in copies:
        copy.wait()


def pack(rows, me, after, chips, first, last, own, left, width):
    ny = rows.shape[1]
    high = (last - first) * width + (ny // chips if left else 0)
    scratch = [pltpu.VMEM((ny, ny), F32), pltpu.VMEM((left * width, ny), F32)] if left else []
    return pl.pallas_call(
        functools.partial(pack_kernel, chips, first, last, own, left, width),
        in_specs=[SMEM, HBM, pl.BlockSpec(memory_space=pl.ANY)],
        out_specs=[VMEM] * chips,
        out_shape=[jax.ShapeDtypeStruct((high, ny), F32)] * chips,
        scratch_shapes=scratch + [pltpu.SemaphoreType.DMA((chips + 1,))],
        compiler_params=PARAMS,
    )(me, pltpu.with_memory_space_constraint(rows, pltpu.HBM), after)


def slabs_of(refs, count, width):
    ny = refs[0].shape[1]
    for s in range(0, count, 2):
        pair = range(s, min(s + 2, count))
        columns = [jnp.concatenate([ref[q * width : (q + 1) * width] for ref in refs], axis=0) for q in pair]
        yield s * ny, (s + len(columns)) * ny, halves(jnp.concatenate(columns, axis=1))


def rest_of(refs, count, left, width):
    blocks = [ref[count * width :] for ref in refs]
    slabs = [[block[:, k * width : (k + 1) * width] for block in blocks] for k in range(left)]
    return halves(jnp.concatenate([jnp.concatenate(parts, axis=1) for parts in slabs], axis=0))


def widen(value, lanes):
    return jnp.concatenate([value, jnp.zeros((value.shape[0], lanes - value.shape[1]), F32)], axis=1)


def project_kernel(count, left, width, me_ref, start_ref, *refs):
    chips, me = (start_ref.shape[1] // width) // 2, me_ref[0]
    refs, (out_ref, high_ref, low_ref, *rest_refs) = refs[:chips], refs[chips:]
    ny = refs[0].shape[1]
    parts = [start_ref[:, i * width : (i + 1) * width] for i in range(2 * chips)]
    odd = (me & 1) != 0
    start = jnp.where(odd, jnp.concatenate(parts[1::2], axis=1), jnp.concatenate(parts[::2], axis=1))
    start = stack(reorder(start, lax.div(me, 2), chips, 1))
    for at, to, slab in slabs_of(refs, count, width):
        out_ref[:, at:to] = dot_split(start, slab, NN)
        high_ref[at // (2 * ny), :, : to - at], low_ref[at // (2 * ny), :, : to - at] = slab
    if left:
        rest = rest_of(refs, count, left, width)
        rest_refs[0][...], rest_refs[1][...] = rest
        out_ref[:, count * ny :] = widen(dot_split(start, rest, NT), ny)


def project(blocks, start_t, me, count, left, width):
    chips, ny = len(blocks), blocks[0].shape[1]
    pairs = jax.ShapeDtypeStruct(((count + 1) // 2, chips * width, 2 * ny), BF16)
    rest = [jax.ShapeDtypeStruct((left * (ny // chips), chips * width), BF16)] * 2 if left else []
    columns = jax.ShapeDtypeStruct((start_t.shape[0], (count + (left > 0)) * ny), F32)
    return pl.pallas_call(
        functools.partial(project_kernel, count, left, width),
        in_specs=[SMEM] + [VMEM] * (1 + chips),
        out_specs=[VMEM] * (3 + len(rest)),
        out_shape=[columns, pairs, pairs] + rest,
        compiler_params=PARAMS,
    )(me, start_t, *blocks)


def split_slabs(high_ref, low_ref, count, ny):
    for s in range(0, count, 2):
        to = min(s + 2, count)
        lanes = slice(0, (to - s) * ny)
        yield s * ny, to * ny, (high_ref[s // 2, :, lanes], low_ref[s // 2, :, lanes])


def raw_kernel(count, ny, chips, last, me_ref, mine_ref, other_ref, high_ref, low_ref, *refs):
    refs, out_ref = refs[:-1], refs[-1]
    total = refs[0][...] if last else jnp.zeros(out_ref.shape, F32)
    for at, to, slab in split_slabs(high_ref, low_ref, count, ny):
        total += dot_split(stack(mine_ref[:, at:to] + other_ref[:, at:to]), slab, NT)
    if last:
        rest = (refs[1][...], refs[2][...])
        lanes = slice(count * ny, count * ny + rest[0].shape[0])
        total += dot_split(stack(mine_ref[:, lanes] + other_ref[:, lanes]), rest, NN)
        total = reorder(total, lax.div(me_ref[0], 2), chips, 1)
    out_ref[...] = total


def raw_part(mine, other, pairs, before, me, count, ny, chips):
    last = before is not None
    args = [me, mine, other, *pairs[:2]] + ([before, *pairs[2:]] if last else [])
    return pl.pallas_call(
        functools.partial(raw_kernel, count, ny, chips, last),
        in_specs=[SMEM] + [VMEM] * (len(args) - 1),
        out_specs=VMEM,
        out_shape=jax.ShapeDtypeStruct((mine.shape[0], pairs[0].shape[1]), F32),
        compiler_params=PARAMS,
    )(*args)


def sum_over(value, axis, low, size):
    while low < size:
        masks = [low] if 2 * low >= size else [low, 2 * low, 3 * low]
        got = [exchange(value, axis, mask, size) for mask in masks]
        for term in got:
            value = value + term
        low *= len(masks) + 1
    return value


def gram_kernel(raw_ref, out_ref):
    raw = raw_ref[...]
    out_ref[...] = lax.dot_general(raw, raw, NT, precision=HIGHEST, preferred_element_type=F32)


def gram_part(raw):
    return pl.pallas_call(
        gram_kernel,
        in_specs=[VMEM],
        out_specs=VMEM,
        out_shape=jax.ShapeDtypeStruct((raw.shape[0], raw.shape[0]), F32),
        compiler_params=PARAMS,
    )(raw)


def inverse_factor(gram):
    rank = gram.shape[0]
    row = lax.broadcasted_iota(jnp.int32, (rank, rank), 0)
    col = lax.broadcasted_iota(jnp.int32, (rank, rank), 1)
    table = jnp.concatenate([gram, jnp.where(row == col, 1.0, 0.0).astype(F32)], axis=1)
    rows = [table[8 * b : 8 * b + 8] for b in range(rank // 8)]
    wide = rows[0].shape
    sub = lax.broadcasted_iota(jnp.int32, wide, 0)

    def spread(value, k):
        return jnp.broadcast_to(value[k : k + 1], wide)

    inverse = []
    for b in range(len(rows)):
        columns = [
            [jnp.broadcast_to(block[:, 8 * b + k : 8 * b + k + 1], wide) for k in range(8)] for block in rows[b:]
        ]
        pivots = jnp.ones(wide, F32)
        for k in range(8):
            pivot = spread(columns[0][k], k)
            pivots = jnp.where(sub == k, pivot, pivots)
            scale = 1.0 / pivot
            across = spread(rows[b], k)
            ahead = [spread(columns[0][m], k) for m in range(k + 1, 8)]
            for i, column in enumerate(columns):
                factor = jnp.where(sub > k, column[k], 0.0) if i == 0 else column[k]
                for m in range(k + 1, 8):
                    column[m] = column[m] - (factor * ahead[m - k - 1]) * scale
                rows[b + i] = rows[b + i] - (factor * across) * scale
        inverse.append(rows[b][:, rank:] * lax.rsqrt(pivots[:, rank:]))
    return jnp.concatenate(inverse, axis=0)


def core_kernel(counts, me_ref, mine_ref, other_ref, raw_ref, *refs):
    refs, (keep_ref, send_ref) = refs[:-2], refs[-2:]
    chips = keep_ref.shape[0]
    each, ny = keep_ref.shape[-2:]
    me = me_ref[0]
    inverse = inverse_factor(mine_ref[...] + other_ref[...])
    inverse = reorder(inverse, me, 2 * chips, 0)
    raw = reorder(raw_ref[...], lax.div(me, 2), chips, 1)
    basis = stack(lax.dot_general(inverse, raw, NN, precision=HIGHEST, preferred_element_type=F32))

    def put(slab, value):
        for k in range(chips):
            keep_ref[k, slab] = value[2 * k * each : (2 * k + 1) * each]
            send_ref[k, slab] = value[(2 * k + 1) * each : (2 * k + 2) * each]

    done = 0
    for c, count in enumerate(counts):
        for at, to, slab in split_slabs(refs[2 * c], refs[2 * c + 1], count, ny):
            value = dot_split(basis, slab, NN)
            for lane in range(0, to - at, ny):
                put(done + (at + lane) // ny, value[:, lane : lane + ny])
        done += count
    put(done, widen(dot_split(basis, (refs[-2][...], refs[-1][...]), NT), ny))


def core(pairs, mine, other, raw, me, counts, chips, each, ny):
    shape = jax.ShapeDtypeStruct((chips, sum(counts) + 1, each, ny), F32)
    return pl.pallas_call(
        functools.partial(core_kernel, counts),
        in_specs=[SMEM] + [VMEM] * (3 + len(pairs)),
        out_specs=[VMEM] * 2,
        out_shape=[shape] * 2,
        compiler_params=PARAMS,
    )(me, mine, other, raw, *pairs)


def add_kernel(keep_ref, got_ref, *outs):
    for k, out in enumerate(outs):
        out[...] = keep_ref[k] + got_ref[k]


def add_parts(keep, got):
    chips = keep.shape[0]
    return pl.pallas_call(
        add_kernel,
        in_specs=[VMEM] * 2,
        out_specs=[VMEM] * chips,
        out_shape=[jax.ShapeDtypeStruct(keep.shape[1:], F32)] * chips,
        compiler_params=PARAMS,
    )(keep, got)


def place_kernel(own, left, cells, me_ref, *refs):
    refs, (out_ref, rest, sems) = refs[:-3], refs[-3:]
    chips = len(refs)
    chip = lax.div(me_ref[0], 2)
    copies = []
    for k, ref in enumerate(refs):
        to = out_ref.at[pl.ds((chip ^ k) * own, own)]
        copies.append(pltpu.make_async_copy(ref.at[pl.ds(0, own)], to, sems.at[k]))
        copies[-1].start()
    for k in range(left):
        parts = [ref[own][:, k * cells : (k + 1) * cells] for ref in refs]
        rest[k] = reorder(jnp.concatenate(parts, axis=1), chip, chips, 1)
    copies.append(pltpu.make_async_copy(rest, out_ref.at[pl.ds(chips * own, left)], sems.at[chips]))
    copies[-1].start()
    for copy in copies:
        copy.wait()


def place(parts, me, own, left):
    chips = len(parts)
    _, each, ny = parts[0].shape
    return pl.pallas_call(
        functools.partial(place_kernel, own, left, ny // chips),
        in_specs=[SMEM] + [VMEM] * chips,
        out_specs=HBM,
        out_shape=jax.ShapeDtypeStruct((chips * own + left, each, ny), F32),
        scratch_shapes=[pltpu.VMEM((left, each, ny), F32), pltpu.SemaphoreType.DMA((chips + 1,))],
        compiler_params=PARAMS,
    )(me, *parts)


def shards(n, layers, field_data, start_block):
    species, planes, width, ny = field_data.shape
    chips, each = n // 2, start_block.shape[1] // n
    total = species * planes
    own, left = divmod(total, chips)
    counts = [own * 5 // 8, own - own * 5 // 8]
    me = lax.axis_index("fib").astype(jnp.int32).reshape(1)
    rows = field_data.reshape(total * width, ny)
    start_t = start_block.T
    pairs, raw, first, after = [], None, 0, me
    for c, count in enumerate(counts):
        rest = left if c == len(counts) - 1 else 0
        sent = pack(rows, me, after, chips, first, first + count, own, rest, width)
        part = [sent[0]] + [exchange(sent[k], "fib", 2 * k, n) for k in range(1, chips)]
        mine, *split = project(part, start_t, me, count, rest, width)
        other = exchange(mine, "fib", 1, n)
        raw = raw_part(mine, other, split, raw, me, count, ny, chips)
        pairs += split
        first += count
        after = sent[0]
    raw = sum_over(sum_over(raw, "fib", 2, n), "blk", 1, layers)
    gram = gram_part(raw)
    keep, send = core(pairs, gram, exchange(gram, "fib", 1, n), raw, me, counts, chips, each, ny)
    parts = add_parts(keep, exchange(send, "fib", 1, n))
    parts = [parts[0]] + [exchange(parts[k], "fib", 2 * k, n) for k in range(1, chips)]
    return place(parts, me, own, left).reshape(species, planes, each, ny)


def solution(mesh):
    n, layers = mesh.shape["fib"], mesh.shape["blk"]
    in_specs = (P(None, "blk", "fib", None), P())
    out_specs = P(None, "blk", "fib", None)
    return jax.shard_map(
        functools.partial(shards, n, layers), mesh=mesh, in_specs=in_specs, out_specs=out_specs, check_vma=False
    )
```

```python
import functools

import jax
import jax.numpy as jnp
from jax import lax
from jax.experimental import pallas as pl
from jax.experimental.pallas import tpu as pltpu
from jax.sharding import PartitionSpec as P

F32, BF16 = jnp.float32, jnp.bfloat16
HIGHEST = lax.Precision.HIGHEST
NN = (((1,), (0,)), ((), ()))
NT = (((1,), (1,)), ((), ()))
PARAMS = pltpu.CompilerParams(vmem_limit_bytes=40 * 1024 * 1024)
VMEM = pl.BlockSpec(memory_space=pltpu.VMEM)
SMEM = pl.BlockSpec(memory_space=pltpu.SMEM)
HBM = pl.BlockSpec(memory_space=pltpu.HBM)


def halves(value):
    high = value.astype(BF16)
    return high, (value - high.astype(F32)).astype(BF16)


def stack(value):
    return jnp.concatenate(halves(value), axis=0)


def dot(left, right, dims):
    return lax.dot_general(left, right, dims, preferred_element_type=F32)


def dot_split(left, right, dims):
    rows = left.shape[0] // 2
    right_high, right_low = right
    both = dot(left, right_high, dims)
    return both[:rows] + both[rows:] + dot(left[:rows], right_low, dims)


def reorder(value, me, n, axis):
    width = value.shape[axis] // n
    bit = 1
    while bit < n:
        parts = [lax.slice_in_dim(value, i * bit * width, (i + 1) * bit * width, axis=axis) for i in range(n // bit)]
        swapped = jnp.concatenate([parts[i ^ 1] for i in range(n // bit)], axis=axis)
        value = jnp.where((me & bit) != 0, swapped, value)
        bit *= 2
    return value


def far_first(masks):
    return [masks[-1], *masks[:-1]]


def for_order(blocks):
    return [blocks[k] for k in [*far_first(range(1, len(blocks))), 0]]


def in_order(refs):
    return [refs[-1], *refs[1:-1], refs[0]]


def exchange(value, axis, mask, size):
    return lax.ppermute(value, axis, [(i, i ^ mask) for i in range(size)])


def pack_kernel(chips, first, last, own, left, width, me_ref, rows_ref, after, *refs):
    del after
    blocks, refs = refs[:chips], refs[chips:]
    ny = rows_ref.shape[1]
    chip = lax.div(me_ref[0], 2)
    sems = refs[-1]
    count = (last - first) * width
    if left:
        turned, rest = refs[:2]
        rest_copy = pltpu.make_async_copy(rows_ref.at[pl.ds(chips * own * width, left * width)], rest, sems.at[chips])
        rest_copy.start()
    copies = []
    for k, block in enumerate(blocks):
        at = pl.multiple_of(((chip ^ k) * own + first) * width, 8)
        copies.append(pltpu.make_async_copy(rows_ref.at[pl.ds(at, count)], block.at[pl.ds(0, count)], sems.at[k]))
        copies[-1].start()
    if left:
        cells = ny // chips
        rest_copy.wait()
        turned[:, : left * width] = rest[...].T
        for k, block in enumerate(blocks):
            block[count:] = turned[pl.ds(pl.multiple_of((chip ^ k) * cells, cells), cells), :]
    for copy in copies:
        copy.wait()


def pack(rows, me, after, chips, first, last, own, left, width):
    ny = rows.shape[1]
    high = (last - first) * width + (ny // chips if left else 0)
    scratch = [pltpu.VMEM((ny, ny), F32), pltpu.VMEM((left * width, ny), F32)] if left else []
    return pl.pallas_call(
        functools.partial(pack_kernel, chips, first, last, own, left, width),
        in_specs=[SMEM, HBM, pl.BlockSpec(memory_space=pl.ANY)],
        out_specs=[VMEM] * chips,
        out_shape=[jax.ShapeDtypeStruct((high, ny), F32)] * chips,
        scratch_shapes=scratch + [pltpu.SemaphoreType.DMA((chips + 1,))],
        compiler_params=PARAMS,
    )(me, pltpu.with_memory_space_constraint(rows, pltpu.HBM), after)


def slabs_of(refs, count, width):
    ny = refs[0].shape[1]
    for s in range(0, count, 2):
        pair = range(s, min(s + 2, count))
        columns = [jnp.concatenate([ref[q * width : (q + 1) * width] for ref in refs], axis=0) for q in pair]
        yield s * ny, (s + len(columns)) * ny, halves(jnp.concatenate(columns, axis=1))


def rest_of(refs, count, left, width):
    blocks = [ref[count * width :] for ref in refs]
    slabs = [[block[:, k * width : (k + 1) * width] for block in blocks] for k in range(left)]
    return halves(jnp.concatenate([jnp.concatenate(parts, axis=1) for parts in slabs], axis=0))


def widen(value, lanes):
    return jnp.concatenate([value, jnp.zeros((value.shape[0], lanes - value.shape[1]), F32)], axis=1)


def project_kernel(count, left, width, me_ref, start_ref, *refs):
    chips, me = (start_ref.shape[1] // width) // 2, me_ref[0]
    refs, (out_ref, high_ref, low_ref, *rest_refs) = in_order(refs[:chips]), refs[chips:]
    ny = refs[0].shape[1]
    parts = [start_ref[:, i * width : (i + 1) * width] for i in range(2 * chips)]
    odd = (me & 1) != 0
    start = jnp.where(odd, jnp.concatenate(parts[1::2], axis=1), jnp.concatenate(parts[::2], axis=1))
    start = stack(reorder(start, lax.div(me, 2), chips, 1))
    for at, to, slab in slabs_of(refs, count, width):
        out_ref[:, at:to] = dot_split(start, slab, NN)
        high_ref[at // (2 * ny), :, : to - at], low_ref[at // (2 * ny), :, : to - at] = slab
    if left:
        rest = rest_of(refs, count, left, width)
        rest_refs[0][...], rest_refs[1][...] = rest
        out_ref[:, count * ny :] = widen(dot_split(start, rest, NT), ny)


def project(blocks, start_t, me, count, left, width):
    chips, ny = len(blocks), blocks[0].shape[1]
    pairs = jax.ShapeDtypeStruct(((count + 1) // 2, chips * width, 2 * ny), BF16)
    rest = [jax.ShapeDtypeStruct((left * (ny // chips), chips * width), BF16)] * 2 if left else []
    columns = jax.ShapeDtypeStruct((start_t.shape[0], (count + (left > 0)) * ny), F32)
    return pl.pallas_call(
        functools.partial(project_kernel, count, left, width),
        in_specs=[SMEM] + [VMEM] * (1 + chips),
        out_specs=[VMEM] * (3 + len(rest)),
        out_shape=[columns, pairs, pairs] + rest,
        compiler_params=PARAMS,
    )(me, start_t, *for_order(blocks))


def split_slabs(high_ref, low_ref, count, ny):
    for s in range(0, count, 2):
        to = min(s + 2, count)
        lanes = slice(0, (to - s) * ny)
        yield s * ny, to * ny, (high_ref[s // 2, :, lanes], low_ref[s // 2, :, lanes])


def raw_kernel(count, ny, chips, last, me_ref, mine_ref, other_ref, high_ref, low_ref, *refs):
    refs, out_ref = refs[:-1], refs[-1]
    total = refs[0][...] if last else jnp.zeros(out_ref.shape, F32)
    for at, to, slab in split_slabs(high_ref, low_ref, count, ny):
        total += dot_split(stack(mine_ref[:, at:to] + other_ref[:, at:to]), slab, NT)
    if last:
        rest = (refs[1][...], refs[2][...])
        lanes = slice(count * ny, count * ny + rest[0].shape[0])
        total += dot_split(stack(mine_ref[:, lanes] + other_ref[:, lanes]), rest, NN)
        total = reorder(total, lax.div(me_ref[0], 2), chips, 1)
    out_ref[...] = total


def raw_part(mine, other, pairs, before, me, count, ny, chips):
    last = before is not None
    args = [me, mine, other, *pairs[:2]] + ([before, *pairs[2:]] if last else [])
    return pl.pallas_call(
        functools.partial(raw_kernel, count, ny, chips, last),
        in_specs=[SMEM] + [VMEM] * (len(args) - 1),
        out_specs=VMEM,
        out_shape=jax.ShapeDtypeStruct((mine.shape[0], pairs[0].shape[1]), F32),
        compiler_params=PARAMS,
    )(*args)


def sum_over(value, axis, low, size):
    while low < size:
        masks = [low] if 2 * low >= size else [low, 2 * low, 3 * low]
        got = [exchange(value, axis, mask, size) for mask in far_first(masks)]
        for term in reversed(got):
            value = value + term
        low *= len(masks) + 1
    return value


def gram_kernel(raw_ref, out_ref):
    raw = raw_ref[...]
    out_ref[...] = lax.dot_general(raw, raw, NT, precision=HIGHEST, preferred_element_type=F32)


def gram_part(raw):
    return pl.pallas_call(
        gram_kernel,
        in_specs=[VMEM],
        out_specs=VMEM,
        out_shape=jax.ShapeDtypeStruct((raw.shape[0], raw.shape[0]), F32),
        compiler_params=PARAMS,
    )(raw)


def inverse_factor(gram):
    rank = gram.shape[0]
    row = lax.broadcasted_iota(jnp.int32, (rank, rank), 0)
    col = lax.broadcasted_iota(jnp.int32, (rank, rank), 1)
    table = jnp.concatenate([gram, jnp.where(row == col, 1.0, 0.0).astype(F32)], axis=1)
    rows = [table[8 * b : 8 * b + 8] for b in range(rank // 8)]
    wide = rows[0].shape
    sub = lax.broadcasted_iota(jnp.int32, wide, 0)

    def spread(value, k):
        return jnp.broadcast_to(value[k : k + 1], wide)

    inverse = []
    for b in range(len(rows)):
        columns = [
            [jnp.broadcast_to(block[:, 8 * b + k : 8 * b + k + 1], wide) for k in range(8)] for block in rows[b:]
        ]
        pivots = jnp.ones(wide, F32)
        for k in range(8):
            pivot = spread(columns[0][k], k)
            pivots = jnp.where(sub == k, pivot, pivots)
            scale = 1.0 / pivot
            across = spread(rows[b], k)
            ahead = [spread(columns[0][m], k) for m in range(k + 1, 8)]
            for i, column in enumerate(columns):
                factor = jnp.where(sub > k, column[k], 0.0) if i == 0 else column[k]
                for m in range(k + 1, 8):
                    column[m] = column[m] - (factor * ahead[m - k - 1]) * scale
                rows[b + i] = rows[b + i] - (factor * across) * scale
        inverse.append(rows[b][:, rank:] * lax.rsqrt(pivots[:, rank:]))
    return jnp.concatenate(inverse, axis=0)


def core_kernel(counts, me_ref, mine_ref, other_ref, raw_ref, *refs):
    refs, (keep_ref, send_ref) = refs[:-2], refs[-2:]
    chips = keep_ref.shape[0]
    each, ny = keep_ref.shape[-2:]
    me = me_ref[0]
    inverse = inverse_factor(mine_ref[...] + other_ref[...])
    inverse = reorder(inverse, me, 2 * chips, 0)
    raw = reorder(raw_ref[...], lax.div(me, 2), chips, 1)
    basis = stack(lax.dot_general(inverse, raw, NN, precision=HIGHEST, preferred_element_type=F32))

    def put(slab, value):
        for k in range(chips):
            keep_ref[k, slab] = value[2 * k * each : (2 * k + 1) * each]
            send_ref[k, slab] = value[(2 * k + 1) * each : (2 * k + 2) * each]

    done = 0
    for c, count in enumerate(counts):
        for at, to, slab in split_slabs(refs[2 * c], refs[2 * c + 1], count, ny):
            value = dot_split(basis, slab, NN)
            for lane in range(0, to - at, ny):
                put(done + (at + lane) // ny, value[:, lane : lane + ny])
        done += count
    put(done, widen(dot_split(basis, (refs[-2][...], refs[-1][...]), NT), ny))


def core(pairs, mine, other, raw, me, counts, chips, each, ny):
    shape = jax.ShapeDtypeStruct((chips, sum(counts) + 1, each, ny), F32)
    return pl.pallas_call(
        functools.partial(core_kernel, counts),
        in_specs=[SMEM] + [VMEM] * (3 + len(pairs)),
        out_specs=[VMEM] * 2,
        out_shape=[shape] * 2,
        compiler_params=PARAMS,
    )(me, mine, other, raw, *pairs)


def add_kernel(keep_ref, got_ref, *outs):
    for k, out in enumerate(outs):
        out[...] = keep_ref[k] + got_ref[k]


def add_parts(keep, got):
    chips = keep.shape[0]
    return pl.pallas_call(
        add_kernel,
        in_specs=[VMEM] * 2,
        out_specs=[VMEM] * chips,
        out_shape=[jax.ShapeDtypeStruct(keep.shape[1:], F32)] * chips,
        compiler_params=PARAMS,
    )(keep, got)


def place_kernel(own, left, cells, me_ref, *refs):
    refs, (out_ref, rest, sems) = refs[:-3], refs[-3:]
    chips = len(refs)
    refs = in_order(refs)
    chip = lax.div(me_ref[0], 2)
    copies = []
    for k, ref in enumerate(refs):
        to = out_ref.at[pl.ds((chip ^ k) * own, own)]
        copies.append(pltpu.make_async_copy(ref.at[pl.ds(0, own)], to, sems.at[k]))
        copies[-1].start()
    for k in range(left):
        parts = [ref[own][:, k * cells : (k + 1) * cells] for ref in refs]
        rest[k] = reorder(jnp.concatenate(parts, axis=1), chip, chips, 1)
    copies.append(pltpu.make_async_copy(rest, out_ref.at[pl.ds(chips * own, left)], sems.at[chips]))
    copies[-1].start()
    for copy in copies:
        copy.wait()


def place(parts, me, own, left):
    chips = len(parts)
    _, each, ny = parts[0].shape
    return pl.pallas_call(
        functools.partial(place_kernel, own, left, ny // chips),
        in_specs=[SMEM] + [VMEM] * chips,
        out_specs=HBM,
        out_shape=jax.ShapeDtypeStruct((chips * own + left, each, ny), F32),
        scratch_shapes=[pltpu.VMEM((left, each, ny), F32), pltpu.SemaphoreType.DMA((chips + 1,))],
        compiler_params=PARAMS,
    )(me, *for_order(parts))


def shards(n, layers, field_data, start_block):
    species, planes, width, ny = field_data.shape
    chips, each = n // 2, start_block.shape[1] // n
    total = species * planes
    own, left = divmod(total, chips)
    counts = [own * 5 // 8, own - own * 5 // 8]
    me = lax.axis_index("fib").astype(jnp.int32).reshape(1)
    rows = field_data.reshape(total * width, ny)
    start_t = start_block.T
    pairs, raw, first, after = [], None, 0, me
    for c, count in enumerate(counts):
        rest = left if c == len(counts) - 1 else 0
        sent = pack(rows, me, after, chips, first, first + count, own, rest, width)
        part = [sent[0]] + [exchange(sent[k], "fib", 2 * k, n) for k in range(1, chips)]
        mine, *split = project(part, start_t, me, count, rest, width)
        other = exchange(mine, "fib", 1, n)
        raw = raw_part(mine, other, split, raw, me, count, ny, chips)
        pairs += split
        first += count
        after = sent[0]
    raw = sum_over(sum_over(raw, "fib", 2, n), "blk", 1, layers)
    gram = gram_part(raw)
    keep, send = core(pairs, gram, exchange(gram, "fib", 1, n), raw, me, counts, chips, each, ny)
    parts = add_parts(keep, exchange(send, "fib", 1, n))
    parts = [parts[0]] + [exchange(parts[k], "fib", 2 * k, n) for k in range(1, chips)]
    return place(parts, me, own, left).reshape(species, planes, each, ny)


def solution(mesh):
    n, layers = mesh.shape["fib"], mesh.shape["blk"]
    in_specs = (P(None, "blk", "fib", None), P())
    out_specs = P(None, "blk", "fib", None)
    return jax.shard_map(
        functools.partial(shards, n, layers), mesh=mesh, in_specs=in_specs, out_specs=out_specs, check_vma=False
    )
```

```python
import functools

import jax
import jax.numpy as jnp
from jax import lax
from jax.experimental import pallas as pl
from jax.experimental.pallas import tpu as pltpu
from jax.sharding import PartitionSpec as P

F32, BF16 = jnp.float32, jnp.bfloat16
HIGHEST = lax.Precision.HIGHEST
NN = (((1,), (0,)), ((), ()))
NT = (((1,), (1,)), ((), ()))
PARAMS = pltpu.CompilerParams(vmem_limit_bytes=40 * 1024 * 1024)
VMEM = pl.BlockSpec(memory_space=pltpu.VMEM)
SMEM = pl.BlockSpec(memory_space=pltpu.SMEM)
HBM = pl.BlockSpec(memory_space=pltpu.HBM)


def halves(value):
    high = value.astype(BF16)
    return high, (value - high.astype(F32)).astype(BF16)


def stack(value):
    return jnp.concatenate(halves(value), axis=0)


def dot(left, right, dims):
    return lax.dot_general(left, right, dims, preferred_element_type=F32)


def dot_split(left, right, dims):
    rows = left.shape[0] // 2
    right_high, right_low = right
    both = dot(left, right_high, dims)
    return both[:rows] + both[rows:] + dot(left[:rows], right_low, dims)


def reorder(value, me, n, axis):
    width = value.shape[axis] // n
    bit = 1
    while bit < n:
        parts = [lax.slice_in_dim(value, i * bit * width, (i + 1) * bit * width, axis=axis) for i in range(n // bit)]
        swapped = jnp.concatenate([parts[i ^ 1] for i in range(n // bit)], axis=axis)
        value = jnp.where((me & bit) != 0, swapped, value)
        bit *= 2
    return value


def far_first(masks):
    return [masks[-1], *masks[:-1]]


def for_order(blocks):
    return [blocks[k] for k in [*far_first(range(1, len(blocks))), 0]]


def in_order(refs):
    return [refs[-1], *refs[1:-1], refs[0]]


def exchange(value, axis, mask, size):
    return lax.ppermute(value, axis, [(i, i ^ mask) for i in range(size)])


def pack_kernel(ks, chips, first, last, own, left, width, me_ref, rows_ref, after, *refs):
    del after
    blocks, refs = refs[: len(ks)], refs[len(ks) :]
    ny = rows_ref.shape[1]
    chip = lax.div(me_ref[0], 2)
    sems = refs[-1]
    count = (last - first) * width
    if left:
        turned, rest = refs[:2]
        rest_copy = pltpu.make_async_copy(rows_ref.at[pl.ds(chips * own * width, left * width)], rest, sems.at[chips])
        rest_copy.start()
    copies = []
    for k, block in zip(ks, blocks):
        at = pl.multiple_of(((chip ^ k) * own + first) * width, 8)
        copies.append(pltpu.make_async_copy(rows_ref.at[pl.ds(at, count)], block.at[pl.ds(0, count)], sems.at[k]))
        copies[-1].start()
    if left:
        cells = ny // chips
        rest_copy.wait()
        turned[:, : left * width] = rest[...].T
        for k, block in zip(ks, blocks):
            block[count:] = turned[pl.ds(pl.multiple_of((chip ^ k) * cells, cells), cells), :]
    for copy in copies:
        copy.wait()


def pack(rows, me, after, ks, chips, first, last, own, left, width):
    ny = rows.shape[1]
    high = (last - first) * width + (ny // chips if left else 0)
    scratch = [pltpu.VMEM((ny, ny), F32), pltpu.VMEM((left * width, ny), F32)] if left else []
    return pl.pallas_call(
        functools.partial(pack_kernel, ks, chips, first, last, own, left, width),
        in_specs=[SMEM, HBM, pl.BlockSpec(memory_space=pl.ANY)],
        out_specs=[VMEM] * len(ks),
        out_shape=[jax.ShapeDtypeStruct((high, ny), F32)] * len(ks),
        scratch_shapes=scratch + [pltpu.SemaphoreType.DMA((chips + 1,))],
        compiler_params=PARAMS,
    )(me, pltpu.with_memory_space_constraint(rows, pltpu.HBM), after)


def slabs_of(refs, count, width):
    ny = refs[0].shape[1]
    for s in range(0, count, 2):
        pair = range(s, min(s + 2, count))
        columns = [jnp.concatenate([ref[q * width : (q + 1) * width] for ref in refs], axis=0) for q in pair]
        yield s * ny, (s + len(columns)) * ny, halves(jnp.concatenate(columns, axis=1))


def rest_of(refs, count, left, width):
    blocks = [ref[count * width :] for ref in refs]
    slabs = [[block[:, k * width : (k + 1) * width] for block in blocks] for k in range(left)]
    return halves(jnp.concatenate([jnp.concatenate(parts, axis=1) for parts in slabs], axis=0))


def widen(value, lanes):
    return jnp.concatenate([value, jnp.zeros((value.shape[0], lanes - value.shape[1]), F32)], axis=1)


def project_kernel(count, left, width, me_ref, start_ref, *refs):
    chips, me = (start_ref.shape[1] // width) // 2, me_ref[0]
    refs, (out_ref, high_ref, low_ref, *rest_refs) = in_order(refs[:chips]), refs[chips:]
    ny = refs[0].shape[1]
    parts = [start_ref[:, i * width : (i + 1) * width] for i in range(2 * chips)]
    odd = (me & 1) != 0
    start = jnp.where(odd, jnp.concatenate(parts[1::2], axis=1), jnp.concatenate(parts[::2], axis=1))
    start = stack(reorder(start, lax.div(me, 2), chips, 1))
    for at, to, slab in slabs_of(refs, count, width):
        out_ref[:, at:to] = dot_split(start, slab, NN)
        high_ref[at // (2 * ny), :, : to - at], low_ref[at // (2 * ny), :, : to - at] = slab
    if left:
        rest = rest_of(refs, count, left, width)
        rest_refs[0][...], rest_refs[1][...] = rest
        out_ref[:, count * ny :] = widen(dot_split(start, rest, NT), ny)


def project(blocks, start_t, me, count, left, width):
    chips, ny = len(blocks), blocks[0].shape[1]
    pairs = jax.ShapeDtypeStruct(((count + 1) // 2, chips * width, 2 * ny), BF16)
    rest = [jax.ShapeDtypeStruct((left * (ny // chips), chips * width), BF16)] * 2 if left else []
    columns = jax.ShapeDtypeStruct((start_t.shape[0], (count + (left > 0)) * ny), F32)
    return pl.pallas_call(
        functools.partial(project_kernel, count, left, width),
        in_specs=[SMEM] + [VMEM] * (1 + chips),
        out_specs=[VMEM] * (3 + len(rest)),
        out_shape=[columns, pairs, pairs] + rest,
        compiler_params=PARAMS,
    )(me, start_t, *for_order(blocks))


def split_slabs(high_ref, low_ref, count, ny):
    for s in range(0, count, 2):
        to = min(s + 2, count)
        lanes = slice(0, (to - s) * ny)
        yield s * ny, to * ny, (high_ref[s // 2, :, lanes], low_ref[s // 2, :, lanes])


def raw_kernel(count, ny, chips, last, me_ref, mine_ref, other_ref, high_ref, low_ref, *refs):
    refs, out_ref = refs[:-1], refs[-1]
    total = refs[0][...] if last else jnp.zeros(out_ref.shape, F32)
    for at, to, slab in split_slabs(high_ref, low_ref, count, ny):
        total += dot_split(stack(mine_ref[:, at:to] + other_ref[:, at:to]), slab, NT)
    if last:
        rest = (refs[1][...], refs[2][...])
        lanes = slice(count * ny, count * ny + rest[0].shape[0])
        total += dot_split(stack(mine_ref[:, lanes] + other_ref[:, lanes]), rest, NN)
        total = reorder(total, lax.div(me_ref[0], 2), chips, 1)
    out_ref[...] = total


def raw_part(mine, other, pairs, before, me, count, ny, chips):
    last = before is not None
    args = [me, mine, other, *pairs[:2]] + ([before, *pairs[2:]] if last else [])
    return pl.pallas_call(
        functools.partial(raw_kernel, count, ny, chips, last),
        in_specs=[SMEM] + [VMEM] * (len(args) - 1),
        out_specs=VMEM,
        out_shape=jax.ShapeDtypeStruct((mine.shape[0], pairs[0].shape[1]), F32),
        compiler_params=PARAMS,
    )(*args)


def sum_over(value, axis, low, size):
    while low < size:
        masks = [low] if 2 * low >= size else [low, 2 * low, 3 * low]
        got = [exchange(value, axis, mask, size) for mask in far_first(masks)]
        for term in reversed(got):
            value = value + term
        low *= len(masks) + 1
    return value


def gram_kernel(raw_ref, out_ref):
    raw = raw_ref[...]
    out_ref[...] = lax.dot_general(raw, raw, NT, precision=HIGHEST, preferred_element_type=F32)


def gram_part(raw):
    return pl.pallas_call(
        gram_kernel,
        in_specs=[VMEM],
        out_specs=VMEM,
        out_shape=jax.ShapeDtypeStruct((raw.shape[0], raw.shape[0]), F32),
        compiler_params=PARAMS,
    )(raw)


def inverse_factor(gram):
    rank = gram.shape[0]
    row = lax.broadcasted_iota(jnp.int32, (rank, rank), 0)
    col = lax.broadcasted_iota(jnp.int32, (rank, rank), 1)
    table = jnp.concatenate([gram, jnp.where(row == col, 1.0, 0.0).astype(F32)], axis=1)
    rows = [table[8 * b : 8 * b + 8] for b in range(rank // 8)]
    wide = rows[0].shape
    sub = lax.broadcasted_iota(jnp.int32, wide, 0)

    def spread(value, k):
        return jnp.broadcast_to(value[k : k + 1], wide)

    inverse = []
    for b in range(len(rows)):
        columns = [
            [jnp.broadcast_to(block[:, 8 * b + k : 8 * b + k + 1], wide) for k in range(8)] for block in rows[b:]
        ]
        pivots = jnp.ones(wide, F32)
        for k in range(8):
            pivot = spread(columns[0][k], k)
            pivots = jnp.where(sub == k, pivot, pivots)
            scale = 1.0 / pivot
            across = spread(rows[b], k)
            ahead = [spread(columns[0][m], k) for m in range(k + 1, 8)]
            for i, column in enumerate(columns):
                factor = jnp.where(sub > k, column[k], 0.0) if i == 0 else column[k]
                for m in range(k + 1, 8):
                    column[m] = column[m] - (factor * ahead[m - k - 1]) * scale
                rows[b + i] = rows[b + i] - (factor * across) * scale
        inverse.append(rows[b][:, rank:] * lax.rsqrt(pivots[:, rank:]))
    return jnp.concatenate(inverse, axis=0)


def factor_kernel(mine_ref, other_ref, out_ref):
    out_ref[...] = inverse_factor(mine_ref[...] + other_ref[...])


def factor(mine, other):
    return pl.pallas_call(
        factor_kernel,
        in_specs=[VMEM] * 2,
        out_specs=VMEM,
        out_shape=jax.ShapeDtypeStruct(mine.shape, F32),
        compiler_params=PARAMS,
        cost_estimate=pl.CostEstimate(flops=10**10, bytes_accessed=1000, transcendentals=0),
    )(mine, other)


def mixed_kernel(counts, chips, ny, after, me_ref, raw_ref, *refs):
    del after
    refs, out_ref = refs[:-1], refs[-1]
    raw = stack(reorder(raw_ref[...], lax.div(me_ref[0], 2), chips, 1))
    done = 0
    for c, count in enumerate(counts):
        for at, to, slab in split_slabs(refs[2 * c], refs[2 * c + 1], count, ny):
            out_ref[:, done + at : done + to] = dot_split(raw, slab, NN)
        done += count * ny
    out_ref[:, done:] = widen(dot_split(raw, (refs[-2][...], refs[-1][...]), NT), ny)


def mixed(raw, pairs, me, after, counts, chips, ny):
    return pl.pallas_call(
        functools.partial(mixed_kernel, counts, chips, ny),
        in_specs=[pl.BlockSpec(memory_space=pl.ANY), SMEM] + [VMEM] * (1 + len(pairs)),
        out_specs=VMEM,
        out_shape=jax.ShapeDtypeStruct((raw.shape[0], (sum(counts) + 1) * ny), F32),
        compiler_params=PARAMS,
    )(after, me, raw, *pairs)


def core_kernel(chips, me_ref, inverse_ref, mine_ref, other_ref, *outs):
    slabs, each, ny = outs[0].shape
    inverse = reorder(inverse_ref[...], me_ref[0], 2 * chips, 0)
    inverse = jnp.concatenate([inverse[2 * k * each : (2 * k + 1) * each] for k in range(chips)], axis=0)
    for s in range(0, slabs, 2):
        to = min(s + 2, slabs)
        both = mine_ref[:, s * ny : to * ny] + other_ref[:, s * ny : to * ny]
        value = lax.dot_general(inverse, both, NN, precision=HIGHEST, preferred_element_type=F32)
        for k in range(chips):
            for slab in range(s, to):
                lanes = slice((slab - s) * ny, (slab - s + 1) * ny)
                outs[k][slab] = value[k * each : (k + 1) * each, lanes]


def core(inverse, mine, other, me, chips, each, ny):
    return pl.pallas_call(
        functools.partial(core_kernel, chips),
        in_specs=[SMEM] + [VMEM] * 3,
        out_specs=[VMEM] * chips,
        out_shape=[jax.ShapeDtypeStruct((mine.shape[1] // ny, each, ny), F32)] * chips,
        compiler_params=PARAMS,
    )(me, inverse, mine, other)


def place_kernel(own, left, cells, me_ref, *refs):
    refs, (out_ref, rest, sems) = refs[:-3], refs[-3:]
    chips = len(refs)
    refs = in_order(refs)
    chip = lax.div(me_ref[0], 2)
    copies = []
    for k, ref in enumerate(refs):
        to = out_ref.at[pl.ds((chip ^ k) * own, own)]
        copies.append(pltpu.make_async_copy(ref.at[pl.ds(0, own)], to, sems.at[k]))
        copies[-1].start()
    for k in range(left):
        parts = [ref[own][:, k * cells : (k + 1) * cells] for ref in refs]
        rest[k] = reorder(jnp.concatenate(parts, axis=1), chip, chips, 1)
    copies.append(pltpu.make_async_copy(rest, out_ref.at[pl.ds(chips * own, left)], sems.at[chips]))
    copies[-1].start()
    for copy in copies:
        copy.wait()


def place(parts, me, own, left):
    chips = len(parts)
    _, each, ny = parts[0].shape
    return pl.pallas_call(
        functools.partial(place_kernel, own, left, ny // chips),
        in_specs=[SMEM] + [VMEM] * chips,
        out_specs=HBM,
        out_shape=jax.ShapeDtypeStruct((chips * own + left, each, ny), F32),
        scratch_shapes=[pltpu.VMEM((left, each, ny), F32), pltpu.SemaphoreType.DMA((chips + 1,))],
        compiler_params=PARAMS,
    )(me, *for_order(parts))


def shards(n, layers, field_data, start_block):
    species, planes, width, ny = field_data.shape
    chips, each = n // 2, start_block.shape[1] // n
    total = species * planes
    own, left = divmod(total, chips)
    counts = [own * 5 // 8, own - own * 5 // 8]
    me = lax.axis_index("fib").astype(jnp.int32).reshape(1)
    rows = field_data.reshape(total * width, ny)
    start_t = start_block.T
    bounds = [(0, counts[0], 0), (counts[0], own, left)]
    near, far = [*range(1, chips - 1)], [chips - 1]
    sent, after = [{}, {}], me
    for c, ks in [(0, far), (0, [0, *near]), (1, [0, *near, *far])]:
        got = pack(rows, me, after, ks, chips, *bounds[c][:2], own, bounds[c][2], width)
        sent[c].update(zip(ks, got))
        after = got[0]
    pairs, raw = [], None
    for c, (first, last, rest) in enumerate(bounds):
        part = [sent[c][0]] + [exchange(sent[c][k], "fib", 2 * k, n) for k in range(1, chips)]
        mine, *split = project(part, start_t, me, last - first, rest, width)
        other = exchange(mine, "fib", 1, n)
        raw = raw_part(mine, other, split, raw, me, last - first, ny, chips)
        pairs += split
    raw = sum_over(sum_over(raw, "fib", 2, n), "blk", 1, layers)
    gram = gram_part(raw)
    sums = mixed(raw, pairs, me, gram, counts, chips, ny)
    inverse = factor(gram, exchange(gram, "fib", 1, n))
    parts = core(inverse, sums, exchange(sums, "fib", 1, n), me, chips, each, ny)
    parts = [parts[0]] + [exchange(parts[k], "fib", 2 * k, n) for k in range(1, chips)]
    return place(parts, me, own, left).reshape(species, planes, each, ny)


def solution(mesh):
    n, layers = mesh.shape["fib"], mesh.shape["blk"]
    in_specs = (P(None, "blk", "fib", None), P())
    out_specs = P(None, "blk", "fib", None)
    return jax.shard_map(
        functools.partial(shards, n, layers), mesh=mesh, in_specs=in_specs, out_specs=out_specs, check_vma=False
    )
```

```python
import functools

import jax
import jax.numpy as jnp
from jax import lax
from jax.experimental import pallas as pl
from jax.experimental.pallas import tpu as pltpu
from jax.sharding import PartitionSpec as P

F32, BF16 = jnp.float32, jnp.bfloat16
HIGHEST = lax.Precision.HIGHEST
NN = (((1,), (0,)), ((), ()))
NT = (((1,), (1,)), ((), ()))
PARAMS = pltpu.CompilerParams(vmem_limit_bytes=40 * 1024 * 1024)
VMEM = pl.BlockSpec(memory_space=pltpu.VMEM)
SMEM = pl.BlockSpec(memory_space=pltpu.SMEM)
HBM = pl.BlockSpec(memory_space=pltpu.HBM)


def halves(value):
    high = value.astype(BF16)
    return high, (value - high.astype(F32)).astype(BF16)


def stack(value):
    return jnp.concatenate(halves(value), axis=0)


def dot(left, right, dims):
    return lax.dot_general(left, right, dims, preferred_element_type=F32)


def dot_split(left, right, dims):
    rows = left.shape[0] // 2
    right_high, right_low = right
    both = dot(left, right_high, dims)
    return both[:rows] + both[rows:] + dot(left[:rows], right_low, dims)


def reorder(value, me, n, axis):
    width = value.shape[axis] // n
    bit = 1
    while bit < n:
        parts = [lax.slice_in_dim(value, i * bit * width, (i + 1) * bit * width, axis=axis) for i in range(n // bit)]
        swapped = jnp.concatenate([parts[i ^ 1] for i in range(n // bit)], axis=axis)
        value = jnp.where((me & bit) != 0, swapped, value)
        bit *= 2
    return value


def far_first(masks):
    return [masks[-1], *masks[:-1]]


def for_order(blocks):
    return [blocks[k] for k in [*far_first(range(1, len(blocks))), 0]]


def in_order(refs):
    return [refs[-1], *refs[1:-1], refs[0]]


def exchange(value, axis, mask, size):
    return lax.ppermute(value, axis, [(i, i ^ mask) for i in range(size)])


def pack_kernel(ks, chips, first, last, own, left, width, me_ref, rows_ref, after, *refs):
    del after
    blocks, refs = refs[: len(ks)], refs[len(ks) :]
    ny = rows_ref.shape[1]
    chip = lax.div(me_ref[0], 2)
    sems = refs[-1]
    count = (last - first) * width
    if left:
        turned, rest = refs[:2]
        rest_copy = pltpu.make_async_copy(rows_ref.at[pl.ds(chips * own * width, left * width)], rest, sems.at[chips])
        rest_copy.start()
    copies = []
    for k, block in zip(ks, blocks):
        at = pl.multiple_of(((chip ^ k) * own + first) * width, 8)
        copies.append(pltpu.make_async_copy(rows_ref.at[pl.ds(at, count)], block.at[pl.ds(0, count)], sems.at[k]))
        copies[-1].start()
    if left:
        cells = ny // chips
        rest_copy.wait()
        turned[:, : left * width] = rest[...].T
        for k, block in zip(ks, blocks):
            block[count:] = turned[pl.ds(pl.multiple_of((chip ^ k) * cells, cells), cells), :]
    for copy in copies:
        copy.wait()


def pack(rows, me, after, ks, chips, first, last, own, left, width):
    ny = rows.shape[1]
    high = (last - first) * width + (ny // chips if left else 0)
    scratch = [pltpu.VMEM((ny, ny), F32), pltpu.VMEM((left * width, ny), F32)] if left else []
    return pl.pallas_call(
        functools.partial(pack_kernel, ks, chips, first, last, own, left, width),
        in_specs=[SMEM, HBM, pl.BlockSpec(memory_space=pl.ANY)],
        out_specs=[VMEM] * len(ks),
        out_shape=[jax.ShapeDtypeStruct((high, ny), F32)] * len(ks),
        scratch_shapes=scratch + [pltpu.SemaphoreType.DMA((chips + 1,))],
        compiler_params=PARAMS,
    )(me, pltpu.with_memory_space_constraint(rows, pltpu.HBM), after)


def slabs_of(refs, count, width):
    ny = refs[0].shape[1]
    for s in range(0, count, 2):
        pair = range(s, min(s + 2, count))
        columns = [jnp.concatenate([ref[q * width : (q + 1) * width] for ref in refs], axis=0) for q in pair]
        yield s * ny, (s + len(columns)) * ny, halves(jnp.concatenate(columns, axis=1))


def rest_of(refs, count, left, width):
    blocks = [ref[count * width :] for ref in refs]
    slabs = [[block[:, k * width : (k + 1) * width] for block in blocks] for k in range(left)]
    return halves(jnp.concatenate([jnp.concatenate(parts, axis=1) for parts in slabs], axis=0))


def widen(value, lanes):
    return jnp.concatenate([value, jnp.zeros((value.shape[0], lanes - value.shape[1]), F32)], axis=1)


def project_kernel(count, left, width, me_ref, start_ref, *refs):
    chips, me = (start_ref.shape[1] // width) // 2, me_ref[0]
    refs, (out_ref, high_ref, low_ref, *rest_refs) = in_order(refs[:chips]), refs[chips:]
    ny = refs[0].shape[1]
    parts = [start_ref[:, i * width : (i + 1) * width] for i in range(2 * chips)]
    odd = (me & 1) != 0
    start = jnp.where(odd, jnp.concatenate(parts[1::2], axis=1), jnp.concatenate(parts[::2], axis=1))
    start = stack(reorder(start, lax.div(me, 2), chips, 1))
    for at, to, slab in slabs_of(refs, count, width):
        out_ref[:, at:to] = dot_split(start, slab, NN)
        high_ref[at // (2 * ny), :, : to - at], low_ref[at // (2 * ny), :, : to - at] = slab
    if left:
        rest = rest_of(refs, count, left, width)
        rest_refs[0][...], rest_refs[1][...] = rest
        out_ref[:, count * ny :] = widen(dot_split(start, rest, NT), ny)


def project(blocks, start_t, me, count, left, width):
    chips, ny = len(blocks), blocks[0].shape[1]
    pairs = jax.ShapeDtypeStruct(((count + 1) // 2, chips * width, 2 * ny), BF16)
    rest = [jax.ShapeDtypeStruct((left * (ny // chips), chips * width), BF16)] * 2 if left else []
    columns = jax.ShapeDtypeStruct((start_t.shape[0], (count + (left > 0)) * ny), F32)
    return pl.pallas_call(
        functools.partial(project_kernel, count, left, width),
        in_specs=[SMEM] + [VMEM] * (1 + chips),
        out_specs=[VMEM] * (3 + len(rest)),
        out_shape=[columns, pairs, pairs] + rest,
        compiler_params=PARAMS,
    )(me, start_t, *for_order(blocks))


def split_slabs(high_ref, low_ref, count, ny):
    for s in range(0, count, 2):
        to = min(s + 2, count)
        lanes = slice(0, (to - s) * ny)
        yield s * ny, to * ny, (high_ref[s // 2, :, lanes], low_ref[s // 2, :, lanes])


def raw_kernel(count, ny, chips, more, rest, last, me_ref, mine_ref, other_ref, high_ref, low_ref, *refs):
    refs, out_ref = refs[:-1], refs[-1]
    total = refs[0][...] if more else jnp.zeros(out_ref.shape, F32)
    for at, to, slab in split_slabs(high_ref, low_ref, count, ny):
        total += dot_split(stack(mine_ref[:, at:to] + other_ref[:, at:to]), slab, NT)
    if rest:
        halves_of_rest = (refs[-2][...], refs[-1][...])
        lanes = slice(count * ny, count * ny + halves_of_rest[0].shape[0])
        total += dot_split(stack(mine_ref[:, lanes] + other_ref[:, lanes]), halves_of_rest, NN)
    if last:
        total = reorder(total, lax.div(me_ref[0], 2), chips, 1)
    out_ref[...] = total


def raw_part(mine, other, split, before, me, count, ny, chips, last):
    pairs, rest = split[:2], split[2:]
    more = [] if before is None else [before]
    args = [me, mine, other, *pairs, *more, *rest]
    return pl.pallas_call(
        functools.partial(raw_kernel, count, ny, chips, bool(more), bool(rest), last),
        in_specs=[SMEM] + [VMEM] * (len(args) - 1),
        out_specs=VMEM,
        out_shape=jax.ShapeDtypeStruct((mine.shape[0], pairs[0].shape[1]), F32),
        compiler_params=PARAMS,
    )(*args)


def sum_over(value, axis, low, size):
    while low < size:
        masks = [low] if 2 * low >= size else [low, 2 * low, 3 * low]
        got = [exchange(value, axis, mask, size) for mask in far_first(masks)]
        for term in reversed(got):
            value = value + term
        low *= len(masks) + 1
    return value


def gram_kernel(raw_ref, out_ref):
    raw = raw_ref[...]
    out_ref[...] = lax.dot_general(raw, raw, NT, precision=HIGHEST, preferred_element_type=F32)


def gram_part(raw):
    return pl.pallas_call(
        gram_kernel,
        in_specs=[VMEM],
        out_specs=VMEM,
        out_shape=jax.ShapeDtypeStruct((raw.shape[0], raw.shape[0]), F32),
        compiler_params=PARAMS,
    )(raw)


def inverse_factor(gram):
    rank = gram.shape[0]
    row = lax.broadcasted_iota(jnp.int32, (rank, rank), 0)
    col = lax.broadcasted_iota(jnp.int32, (rank, rank), 1)
    table = jnp.concatenate([gram, jnp.where(row == col, 1.0, 0.0).astype(F32)], axis=1)
    count = rank // 8
    rows = [table[8 * b : 8 * b + 8] for b in range(count)]
    wide = rows[0].shape
    sub = lax.broadcasted_iota(jnp.int32, wide, 0)

    def spread(value, k):
        return jnp.broadcast_to(value[k : k + 1], wide)

    def panel(i, b):
        return [jnp.broadcast_to(rows[i][:, 8 * b + k : 8 * b + k + 1], wide) for k in range(8)]

    inverse = []
    head = panel(0, 0)
    for b in range(count):
        below = {i: panel(i, b) for i in range(b + 1, count)}
        side, following = (panel(b, b + 1), panel(b + 1, b + 1)) if below else ([], [])
        pivots = jnp.ones(wide, F32)
        for k in range(8):
            pivot = spread(head[k], k)
            pivots = jnp.where(sub == k, pivot, pivots)
            scale = 1.0 / pivot
            factor = jnp.where(sub > k, head[k], 0.0)
            ahead = [spread(column, k) for column in head[k + 1 :]]
            head[k + 1 :] = [column - (factor * term) * scale for column, term in zip(head[k + 1 :], ahead)]
            factor = factor * scale
            across, beyond = spread(rows[b], k), [spread(column, k) for column in side]
            rows[b] = rows[b] - factor * across
            side = [column - factor * term for column, term in zip(side, beyond)]
            for i, columns in below.items():
                factor = columns[k] * scale
                columns[k + 1 :] = [column - factor * term for column, term in zip(columns[k + 1 :], ahead)]
                rows[i] = rows[i] - factor * across
                if i == b + 1:
                    following = [column - factor * term for column, term in zip(following, beyond)]
        inverse.append(rows[b][:, rank:] * lax.rsqrt(pivots[:, rank:]))
        head = following
    return jnp.concatenate(inverse, axis=0)


def factor_kernel(mine_ref, other_ref, out_ref):
    out_ref[...] = inverse_factor(mine_ref[...] + other_ref[...])


def factor(mine, other):
    return pl.pallas_call(
        factor_kernel,
        in_specs=[VMEM] * 2,
        out_specs=VMEM,
        out_shape=jax.ShapeDtypeStruct(mine.shape, F32),
        compiler_params=PARAMS,
        cost_estimate=pl.CostEstimate(flops=10**10, bytes_accessed=1000, transcendentals=0),
    )(mine, other)


def mixed_kernel(counts, chips, ny, after, me_ref, raw_ref, *refs):
    del after
    refs, out_ref = refs[:-1], refs[-1]
    raw = stack(reorder(raw_ref[...], lax.div(me_ref[0], 2), chips, 1))
    done = 0
    for c, count in enumerate(counts):
        for at, to, slab in split_slabs(refs[2 * c], refs[2 * c + 1], count, ny):
            out_ref[:, done + at : done + to] = dot_split(raw, slab, NN)
        done += count * ny
    out_ref[:, done:] = widen(dot_split(raw, (refs[-2][...], refs[-1][...]), NT), ny)


def mixed(raw, pairs, me, after, counts, chips, ny):
    return pl.pallas_call(
        functools.partial(mixed_kernel, counts, chips, ny),
        in_specs=[pl.BlockSpec(memory_space=pl.ANY), SMEM] + [VMEM] * (1 + len(pairs)),
        out_specs=VMEM,
        out_shape=jax.ShapeDtypeStruct((raw.shape[0], (sum(counts) + 1) * ny), F32),
        compiler_params=PARAMS,
    )(after, me, raw, *pairs)


def core_kernel(chips, me_ref, inverse_ref, mine_ref, other_ref, *outs):
    slabs, each, ny = outs[0].shape
    inverse = reorder(inverse_ref[...], me_ref[0], 2 * chips, 0)
    inverse = jnp.concatenate([inverse[2 * k * each : (2 * k + 1) * each] for k in range(chips)], axis=0)
    for s in range(0, slabs, 2):
        to = min(s + 2, slabs)
        both = mine_ref[:, s * ny : to * ny] + other_ref[:, s * ny : to * ny]
        value = lax.dot_general(inverse, both, NN, precision=HIGHEST, preferred_element_type=F32)
        for k in range(chips):
            for slab in range(s, to):
                lanes = slice((slab - s) * ny, (slab - s + 1) * ny)
                outs[k][slab] = value[k * each : (k + 1) * each, lanes]


def core(inverse, mine, other, me, chips, each, ny):
    return pl.pallas_call(
        functools.partial(core_kernel, chips),
        in_specs=[SMEM] + [VMEM] * 3,
        out_specs=[VMEM] * chips,
        out_shape=[jax.ShapeDtypeStruct((mine.shape[1] // ny, each, ny), F32)] * chips,
        compiler_params=PARAMS,
    )(me, inverse, mine, other)


def place_kernel(own, left, cells, me_ref, *refs):
    refs, (out_ref, rest, sems) = refs[:-3], refs[-3:]
    chips = len(refs)
    refs = in_order(refs)
    chip = lax.div(me_ref[0], 2)
    copies = []
    for k, ref in enumerate(refs):
        to = out_ref.at[pl.ds((chip ^ k) * own, own)]
        copies.append(pltpu.make_async_copy(ref.at[pl.ds(0, own)], to, sems.at[k]))
        copies[-1].start()
    for k in range(left):
        parts = [ref[own][:, k * cells : (k + 1) * cells] for ref in refs]
        rest[k] = reorder(jnp.concatenate(parts, axis=1), chip, chips, 1)
    copies.append(pltpu.make_async_copy(rest, out_ref.at[pl.ds(chips * own, left)], sems.at[chips]))
    copies[-1].start()
    for copy in copies:
        copy.wait()


def place(parts, me, own, left):
    chips = len(parts)
    _, each, ny = parts[0].shape
    return pl.pallas_call(
        functools.partial(place_kernel, own, left, ny // chips),
        in_specs=[SMEM] + [VMEM] * chips,
        out_specs=HBM,
        out_shape=jax.ShapeDtypeStruct((chips * own + left, each, ny), F32),
        scratch_shapes=[pltpu.VMEM((left, each, ny), F32), pltpu.SemaphoreType.DMA((chips + 1,))],
        compiler_params=PARAMS,
    )(me, *for_order(parts))


def shards(n, layers, field_data, start_block):
    species, planes, width, ny = field_data.shape
    chips, each = n // 2, start_block.shape[1] // n
    total = species * planes
    own, left = divmod(total, chips)
    counts = [own * 3 // 8, own * 3 // 8]
    counts.append(own - sum(counts))
    me = lax.axis_index("fib").astype(jnp.int32).reshape(1)
    rows = field_data.reshape(total * width, ny)
    start_t = start_block.T
    bounds, first = [], 0
    for c, count in enumerate(counts):
        bounds.append((first, first + count, left if c == 1 else 0))
        first += count
    near, far = [*range(1, chips - 1)], [chips - 1]
    sent, after = [{} for _ in counts], me
    for c, ks in [(0, far), (0, [0, *near]), (1, [0, *near, *far]), (2, [0, *near, *far])]:
        got = pack(rows, me, after, ks, chips, *bounds[c][:2], own, bounds[c][2], width)
        sent[c].update(zip(ks, got))
        after = got[0]
    pairs, rests, raw = [], [], None
    for c, (first, last, rest) in enumerate(bounds):
        part = [sent[c][0]] + [exchange(sent[c][k], "fib", 2 * k, n) for k in range(1, chips)]
        mine, *split = project(part, start_t, me, last - first, rest, width)
        other = exchange(mine, "fib", 1, n)
        raw = raw_part(mine, other, split, raw, me, last - first, ny, chips, last == own)
        pairs += split[:2]
        rests += split[2:]
    raw = sum_over(sum_over(raw, "fib", 2, n), "blk", 1, layers)
    gram = gram_part(raw)
    sums = mixed(raw, pairs + rests, me, gram, counts, chips, ny)
    inverse = factor(gram, exchange(gram, "fib", 1, n))
    parts = core(inverse, sums, exchange(sums, "fib", 1, n), me, chips, each, ny)
    parts = [parts[0]] + [exchange(parts[k], "fib", 2 * k, n) for k in range(1, chips)]
    return place(parts, me, own, left).reshape(species, planes, each, ny)


def solution(mesh):
    n, layers = mesh.shape["fib"], mesh.shape["blk"]
    in_specs = (P(None, "blk", "fib", None), P())
    out_specs = P(None, "blk", "fib", None)
    return jax.shard_map(
        functools.partial(shards, n, layers), mesh=mesh, in_specs=in_specs, out_specs=out_specs, check_vma=False
    )
```

```python
import functools

import jax
import jax.numpy as jnp
from jax import lax
from jax.experimental import pallas as pl
from jax.experimental.pallas import tpu as pltpu
from jax.sharding import PartitionSpec as P

F32, BF16 = jnp.float32, jnp.bfloat16
HIGHEST = lax.Precision.HIGHEST
NN = (((1,), (0,)), ((), ()))
NT = (((1,), (1,)), ((), ()))
PARAMS = pltpu.CompilerParams(vmem_limit_bytes=40 * 1024 * 1024)
VMEM = pl.BlockSpec(memory_space=pltpu.VMEM)
SMEM = pl.BlockSpec(memory_space=pltpu.SMEM)
HBM = pl.BlockSpec(memory_space=pltpu.HBM)


def halves(value):
    high = value.astype(BF16)
    return high, (value - high.astype(F32)).astype(BF16)


def stack(value):
    return jnp.concatenate(halves(value), axis=0)


def dot(left, right, dims):
    return lax.dot_general(left, right, dims, preferred_element_type=F32)


def dot_split(left, right, dims):
    rows = left.shape[0] // 2
    right_high, right_low = right
    both = dot(left, right_high, dims)
    return both[:rows] + both[rows:] + dot(left[:rows], right_low, dims)


def reorder(value, me, n, axis):
    width = value.shape[axis] // n
    bit = 1
    while bit < n:
        parts = [lax.slice_in_dim(value, i * bit * width, (i + 1) * bit * width, axis=axis) for i in range(n // bit)]
        swapped = jnp.concatenate([parts[i ^ 1] for i in range(n // bit)], axis=axis)
        value = jnp.where((me & bit) != 0, swapped, value)
        bit *= 2
    return value


def far_first(masks):
    return [masks[-1], *masks[:-1]]


def for_order(blocks):
    return [blocks[k] for k in [*far_first(range(1, len(blocks))), 0]]


def in_order(refs):
    return [refs[-1], *refs[1:-1], refs[0]]


def exchange(value, axis, mask, size):
    return lax.ppermute(value, axis, [(i, i ^ mask) for i in range(size)])


def pack_kernel(ks, chips, first, last, own, left, width, me_ref, rows_ref, after, *refs):
    del after
    blocks, refs = refs[: len(ks)], refs[len(ks) :]
    ny = rows_ref.shape[1]
    chip = lax.div(me_ref[0], 2)
    sems = refs[-1]
    count = (last - first) * width
    if left:
        turned, rest = refs[:2]
        rest_copy = pltpu.make_async_copy(rows_ref.at[pl.ds(chips * own * width, left * width)], rest, sems.at[chips])
        rest_copy.start()
    copies = []
    for k, block in zip(ks, blocks):
        at = pl.multiple_of(((chip ^ k) * own + first) * width, 8)
        copies.append(pltpu.make_async_copy(rows_ref.at[pl.ds(at, count)], block.at[pl.ds(0, count)], sems.at[k]))
        copies[-1].start()
    if left:
        cells = ny // chips
        rest_copy.wait()
        turned[:, : left * width] = rest[...].T
        for k, block in zip(ks, blocks):
            block[count:] = turned[pl.ds(pl.multiple_of((chip ^ k) * cells, cells), cells), :]
    for copy in copies:
        copy.wait()


def pack(rows, me, after, ks, chips, first, last, own, left, width):
    ny = rows.shape[1]
    high = (last - first) * width + (ny // chips if left else 0)
    scratch = [pltpu.VMEM((ny, ny), F32), pltpu.VMEM((left * width, ny), F32)] if left else []
    return pl.pallas_call(
        functools.partial(pack_kernel, ks, chips, first, last, own, left, width),
        in_specs=[SMEM, HBM, pl.BlockSpec(memory_space=pl.ANY)],
        out_specs=[VMEM] * len(ks),
        out_shape=[jax.ShapeDtypeStruct((high, ny), F32)] * len(ks),
        scratch_shapes=scratch + [pltpu.SemaphoreType.DMA((chips + 1,))],
        compiler_params=PARAMS,
    )(me, pltpu.with_memory_space_constraint(rows, pltpu.HBM), after)


def slabs_of(refs, count, width):
    ny = refs[0].shape[1]
    for s in range(0, count, 2):
        pair = range(s, min(s + 2, count))
        columns = [jnp.concatenate([ref[q * width : (q + 1) * width] for ref in refs], axis=0) for q in pair]
        yield s * ny, (s + len(columns)) * ny, halves(jnp.concatenate(columns, axis=1))


def rest_of(refs, count, left, width):
    blocks = [ref[count * width :] for ref in refs]
    slabs = [[block[:, k * width : (k + 1) * width] for block in blocks] for k in range(left)]
    return halves(jnp.concatenate([jnp.concatenate(parts, axis=1) for parts in slabs], axis=0))


def widen(value, lanes):
    return jnp.concatenate([value, jnp.zeros((value.shape[0], lanes - value.shape[1]), F32)], axis=1)


def project_kernel(count, left, width, me_ref, start_ref, *refs):
    chips, me = (start_ref.shape[1] // width) // 2, me_ref[0]
    refs, (out_ref, high_ref, low_ref, *rest_refs) = in_order(refs[:chips]), refs[chips:]
    ny = refs[0].shape[1]
    parts = [start_ref[:, i * width : (i + 1) * width] for i in range(2 * chips)]
    odd = (me & 1) != 0
    start = jnp.where(odd, jnp.concatenate(parts[1::2], axis=1), jnp.concatenate(parts[::2], axis=1))
    start = stack(reorder(start, lax.div(me, 2), chips, 1))
    for at, to, slab in slabs_of(refs, count, width):
        out_ref[:, at:to] = dot_split(start, slab, NN)
        high_ref[at // (2 * ny), :, : to - at], low_ref[at // (2 * ny), :, : to - at] = slab
    if left:
        rest = rest_of(refs, count, left, width)
        rest_refs[0][...], rest_refs[1][...] = rest
        out_ref[:, count * ny :] = widen(dot_split(start, rest, NT), ny)


def project(blocks, start_t, me, count, left, width):
    chips, ny = len(blocks), blocks[0].shape[1]
    pairs = jax.ShapeDtypeStruct(((count + 1) // 2, chips * width, 2 * ny), BF16)
    rest = [jax.ShapeDtypeStruct((left * (ny // chips), chips * width), BF16)] * 2 if left else []
    columns = jax.ShapeDtypeStruct((start_t.shape[0], (count + (left > 0)) * ny), F32)
    return pl.pallas_call(
        functools.partial(project_kernel, count, left, width),
        in_specs=[SMEM] + [VMEM] * (1 + chips),
        out_specs=[VMEM] * (3 + len(rest)),
        out_shape=[columns, pairs, pairs] + rest,
        compiler_params=PARAMS,
    )(me, start_t, *for_order(blocks))


def split_slabs(high_ref, low_ref, count, ny):
    for s in range(0, count, 2):
        to = min(s + 2, count)
        lanes = slice(0, (to - s) * ny)
        yield s * ny, to * ny, (high_ref[s // 2, :, lanes], low_ref[s // 2, :, lanes])


def raw_kernel(count, ny, chips, more, rest, last, me_ref, mine_ref, other_ref, high_ref, low_ref, *refs):
    refs, out_ref = refs[:-1], refs[-1]
    total = refs[0][...] if more else jnp.zeros(out_ref.shape, F32)
    for at, to, slab in split_slabs(high_ref, low_ref, count, ny):
        total += dot_split(stack(mine_ref[:, at:to] + other_ref[:, at:to]), slab, NT)
    if rest:
        halves_of_rest = (refs[-2][...], refs[-1][...])
        lanes = slice(count * ny, count * ny + halves_of_rest[0].shape[0])
        total += dot_split(stack(mine_ref[:, lanes] + other_ref[:, lanes]), halves_of_rest, NN)
    if last:
        total = reorder(total, lax.div(me_ref[0], 2), chips, 1)
    out_ref[...] = total


def raw_part(mine, other, split, before, me, count, ny, chips, last):
    pairs, rest = split[:2], split[2:]
    more = [] if before is None else [before]
    args = [me, mine, other, *pairs, *more, *rest]
    return pl.pallas_call(
        functools.partial(raw_kernel, count, ny, chips, bool(more), bool(rest), last),
        in_specs=[SMEM] + [VMEM] * (len(args) - 1),
        out_specs=VMEM,
        out_shape=jax.ShapeDtypeStruct((mine.shape[0], pairs[0].shape[1]), F32),
        compiler_params=PARAMS,
    )(*args)


def sum_over(value, axis, low, size):
    while low < size:
        masks = [low] if 2 * low >= size else [low, 2 * low, 3 * low]
        got = [exchange(value, axis, mask, size) for mask in far_first(masks)]
        for term in reversed(got):
            value = value + term
        low *= len(masks) + 1
    return value


def gram_kernel(raw_ref, out_ref):
    raw = raw_ref[...]
    out_ref[...] = lax.dot_general(raw, raw, NT, precision=HIGHEST, preferred_element_type=F32)


def gram_part(raw):
    return pl.pallas_call(
        gram_kernel,
        in_specs=[VMEM],
        out_specs=VMEM,
        out_shape=jax.ShapeDtypeStruct((raw.shape[0], raw.shape[0]), F32),
        compiler_params=PARAMS,
    )(raw)


def inverse_factor(gram):
    rank = gram.shape[0]
    row = lax.broadcasted_iota(jnp.int32, (rank, rank), 0)
    col = lax.broadcasted_iota(jnp.int32, (rank, rank), 1)
    table = jnp.concatenate([gram, jnp.where(row == col, 1.0, 0.0).astype(F32)], axis=1)
    count = rank // 8
    rows = [table[8 * b : 8 * b + 8] for b in range(count)]
    wide = rows[0].shape
    sub = lax.broadcasted_iota(jnp.int32, wide, 0)

    def spread(value, k):
        return jnp.broadcast_to(value[k : k + 1], wide)

    def panel(i, b):
        return [jnp.broadcast_to(rows[i][:, 8 * b + k : 8 * b + k + 1], wide) for k in range(8)]

    inverse = []
    head = panel(0, 0)
    for b in range(count):
        below = {i: panel(i, b) for i in range(b + 1, count)}
        side, following = (panel(b, b + 1), panel(b + 1, b + 1)) if below else ([], [])
        pivots = jnp.ones(wide, F32)
        for k in range(8):
            pivot = spread(head[k], k)
            pivots = jnp.where(sub == k, pivot, pivots)
            scale = 1.0 / pivot
            factor = jnp.where(sub > k, head[k], 0.0)
            ahead = [spread(column, k) for column in head[k + 1 :]]
            head[k + 1 :] = [column - (factor * term) * scale for column, term in zip(head[k + 1 :], ahead)]
            factor = factor * scale
            across, beyond = spread(rows[b], k), [spread(column, k) for column in side]
            rows[b] = rows[b] - factor * across
            side = [column - factor * term for column, term in zip(side, beyond)]
            for i, columns in below.items():
                factor = columns[k] * scale
                columns[k + 1 :] = [column - factor * term for column, term in zip(columns[k + 1 :], ahead)]
                rows[i] = rows[i] - factor * across
                if i == b + 1:
                    following = [column - factor * term for column, term in zip(following, beyond)]
        inverse.append(rows[b][:, rank:] * lax.rsqrt(pivots[:, rank:]))
        head = following
    return jnp.concatenate(inverse, axis=0)


def factor_kernel(mine_ref, other_ref, out_ref):
    out_ref[...] = inverse_factor(mine_ref[...] + other_ref[...])


def factor(mine, other):
    return pl.pallas_call(
        factor_kernel,
        in_specs=[VMEM] * 2,
        out_specs=VMEM,
        out_shape=jax.ShapeDtypeStruct(mine.shape, F32),
        compiler_params=PARAMS,
        cost_estimate=pl.CostEstimate(flops=10**10, bytes_accessed=1000, transcendentals=0),
    )(mine, other)


def mixed_kernel(counts, chips, ny, after, me_ref, raw_ref, *refs):
    del after
    refs, out_ref = refs[:-1], refs[-1]
    raw = stack(reorder(raw_ref[...], lax.div(me_ref[0], 2), chips, 1))
    done = 0
    for c, count in enumerate(counts):
        for at, to, slab in split_slabs(refs[2 * c], refs[2 * c + 1], count, ny):
            out_ref[:, done + at : done + to] = dot_split(raw, slab, NN)
        done += count * ny
    out_ref[:, done:] = widen(dot_split(raw, (refs[-2][...], refs[-1][...]), NT), ny)


def mixed(raw, pairs, me, after, counts, chips, ny):
    return pl.pallas_call(
        functools.partial(mixed_kernel, counts, chips, ny),
        in_specs=[pl.BlockSpec(memory_space=pl.ANY), SMEM] + [VMEM] * (1 + len(pairs)),
        out_specs=VMEM,
        out_shape=jax.ShapeDtypeStruct((raw.shape[0], (sum(counts) + 1) * ny), F32),
        compiler_params=PARAMS,
    )(after, me, raw, *pairs)


def core_kernel(chips, me_ref, inverse_ref, mine_ref, other_ref, *outs):
    slabs, each, ny = outs[0].shape
    inverse = reorder(inverse_ref[...], me_ref[0], 2 * chips, 0)
    inverse = stack(jnp.concatenate([inverse[2 * k * each : (2 * k + 1) * each] for k in range(chips)], axis=0))
    for s in range(0, slabs, 2):
        to = min(s + 2, slabs)
        both = mine_ref[:, s * ny : to * ny] + other_ref[:, s * ny : to * ny]
        value = dot_split(inverse, halves(both), NN)
        for k in range(chips):
            for slab in range(s, to):
                lanes = slice((slab - s) * ny, (slab - s + 1) * ny)
                outs[k][slab] = value[k * each : (k + 1) * each, lanes]


def core(inverse, mine, other, me, chips, each, ny):
    return pl.pallas_call(
        functools.partial(core_kernel, chips),
        in_specs=[SMEM] + [VMEM] * 3,
        out_specs=[VMEM] * chips,
        out_shape=[jax.ShapeDtypeStruct((mine.shape[1] // ny, each, ny), F32)] * chips,
        compiler_params=PARAMS,
    )(me, inverse, mine, other)


def place_kernel(own, left, cells, me_ref, *refs):
    refs, (out_ref, rest, sems) = refs[:-3], refs[-3:]
    chips = len(refs)
    refs = in_order(refs)
    chip = lax.div(me_ref[0], 2)
    copies = []
    for k, ref in enumerate(refs):
        to = out_ref.at[pl.ds((chip ^ k) * own, own)]
        copies.append(pltpu.make_async_copy(ref.at[pl.ds(0, own)], to, sems.at[k]))
        copies[-1].start()
    for k in range(left):
        parts = [ref[own][:, k * cells : (k + 1) * cells] for ref in refs]
        rest[k] = reorder(jnp.concatenate(parts, axis=1), chip, chips, 1)
    copies.append(pltpu.make_async_copy(rest, out_ref.at[pl.ds(chips * own, left)], sems.at[chips]))
    copies[-1].start()
    for copy in copies:
        copy.wait()


def place(parts, me, own, left):
    chips = len(parts)
    _, each, ny = parts[0].shape
    return pl.pallas_call(
        functools.partial(place_kernel, own, left, ny // chips),
        in_specs=[SMEM] + [VMEM] * chips,
        out_specs=HBM,
        out_shape=jax.ShapeDtypeStruct((chips * own + left, each, ny), F32),
        scratch_shapes=[pltpu.VMEM((left, each, ny), F32), pltpu.SemaphoreType.DMA((chips + 1,))],
        compiler_params=PARAMS,
    )(me, *for_order(parts))


def shards(n, layers, field_data, start_block):
    species, planes, width, ny = field_data.shape
    chips, each = n // 2, start_block.shape[1] // n
    total = species * planes
    own, left = divmod(total, chips)
    counts = [own * 3 // 8, own * 3 // 8]
    counts.append(own - sum(counts))
    me = lax.axis_index("fib").astype(jnp.int32).reshape(1)
    rows = field_data.reshape(total * width, ny)
    start_t = start_block.T
    bounds, first = [], 0
    for c, count in enumerate(counts):
        bounds.append((first, first + count, left if c == 1 else 0))
        first += count
    near, far = [*range(1, chips - 1)], [chips - 1]
    sent, after = [{} for _ in counts], me
    for c, ks in [(0, far), (0, [0, *near]), (1, [0, *near, *far]), (2, [0, *near, *far])]:
        got = pack(rows, me, after, ks, chips, *bounds[c][:2], own, bounds[c][2], width)
        sent[c].update(zip(ks, got))
        after = got[0]
    pairs, rests, raw = [], [], None
    for c, (first, last, rest) in enumerate(bounds):
        part = [sent[c][0]] + [exchange(sent[c][k], "fib", 2 * k, n) for k in range(1, chips)]
        mine, *split = project(part, start_t, me, last - first, rest, width)
        other = exchange(mine, "fib", 1, n)
        raw = raw_part(mine, other, split, raw, me, last - first, ny, chips, last == own)
        pairs += split[:2]
        rests += split[2:]
    raw = sum_over(sum_over(raw, "fib", 2, n), "blk", 1, layers)
    gram = gram_part(raw)
    sums = mixed(raw, pairs + rests, me, gram, counts, chips, ny)
    inverse = factor(gram, exchange(gram, "fib", 1, n))
    parts = core(inverse, sums, exchange(sums, "fib", 1, n), me, chips, each, ny)
    parts = [parts[0]] + [exchange(parts[k], "fib", 2 * k, n) for k in range(1, chips)]
    return place(parts, me, own, left).reshape(species, planes, each, ny)


def solution(mesh):
    n, layers = mesh.shape["fib"], mesh.shape["blk"]
    in_specs = (P(None, "blk", "fib", None), P())
    out_specs = P(None, "blk", "fib", None)
    return jax.shard_map(
        functools.partial(shards, n, layers), mesh=mesh, in_specs=in_specs, out_specs=out_specs, check_vma=False
    )
```

```python
import functools

import jax
import jax.numpy as jnp
from jax import lax
from jax.experimental import pallas as pl
from jax.experimental.pallas import tpu as pltpu
from jax.sharding import PartitionSpec as P

F32, BF16 = jnp.float32, jnp.bfloat16
HIGHEST = lax.Precision.HIGHEST
NN = (((1,), (0,)), ((), ()))
NT = (((1,), (1,)), ((), ()))
PARAMS = pltpu.CompilerParams(vmem_limit_bytes=40 * 1024 * 1024)
VMEM = pl.BlockSpec(memory_space=pltpu.VMEM)
SMEM = pl.BlockSpec(memory_space=pltpu.SMEM)
HBM = pl.BlockSpec(memory_space=pltpu.HBM)


def halves(value):
    high = value.astype(BF16)
    return high, (value - high.astype(F32)).astype(BF16)


def stack(value):
    return jnp.concatenate(halves(value), axis=0)


def dot(left, right, dims):
    return lax.dot_general(left, right, dims, preferred_element_type=F32)


def dot_split(left, right, dims):
    rows = left.shape[0] // 2
    right_high, right_low = right
    both = dot(left, right_high, dims)
    return both[:rows] + both[rows:] + dot(left[:rows], right_low, dims)


def reorder(value, me, n, axis):
    width = value.shape[axis] // n
    bit = 1
    while bit < n:
        parts = [lax.slice_in_dim(value, i * bit * width, (i + 1) * bit * width, axis=axis) for i in range(n // bit)]
        swapped = jnp.concatenate([parts[i ^ 1] for i in range(n // bit)], axis=axis)
        value = jnp.where((me & bit) != 0, swapped, value)
        bit *= 2
    return value


def far_first(masks):
    return [masks[-1], *masks[:-1]]


def for_order(blocks):
    return [blocks[k] for k in [*far_first(range(1, len(blocks))), 0]]


def in_order(refs):
    return [refs[-1], *refs[1:-1], refs[0]]


def exchange(value, axis, mask, size):
    return lax.ppermute(value, axis, [(i, i ^ mask) for i in range(size)])


def pack_kernel(ks, chips, first, last, own, left, width, me_ref, rows_ref, after, *refs):
    del after
    blocks, refs = refs[: len(ks)], refs[len(ks) :]
    ny = rows_ref.shape[1]
    chip = lax.div(me_ref[0], 2)
    sems = refs[-1]
    count = (last - first) * width
    if left:
        turned, rest = refs[:2]
        rest_copy = pltpu.make_async_copy(rows_ref.at[pl.ds(chips * own * width, left * width)], rest, sems.at[chips])
        rest_copy.start()
    copies = []
    for k, block in zip(ks, blocks):
        at = pl.multiple_of(((chip ^ k) * own + first) * width, 8)
        copies.append(pltpu.make_async_copy(rows_ref.at[pl.ds(at, count)], block.at[pl.ds(0, count)], sems.at[k]))
        copies[-1].start()
    if left:
        cells = ny // chips
        rest_copy.wait()
        turned[:, : left * width] = rest[...].T
        for k, block in zip(ks, blocks):
            block[count:] = turned[pl.ds(pl.multiple_of((chip ^ k) * cells, cells), cells), :]
    for copy in copies:
        copy.wait()


def pack(rows, me, after, ks, chips, first, last, own, left, width):
    ny = rows.shape[1]
    high = (last - first) * width + (ny // chips if left else 0)
    scratch = [pltpu.VMEM((ny, ny), F32), pltpu.VMEM((left * width, ny), F32)] if left else []
    return pl.pallas_call(
        functools.partial(pack_kernel, ks, chips, first, last, own, left, width),
        in_specs=[SMEM, HBM, pl.BlockSpec(memory_space=pl.ANY)],
        out_specs=[VMEM] * len(ks),
        out_shape=[jax.ShapeDtypeStruct((high, ny), F32)] * len(ks),
        scratch_shapes=scratch + [pltpu.SemaphoreType.DMA((chips + 1,))],
        compiler_params=PARAMS,
    )(me, pltpu.with_memory_space_constraint(rows, pltpu.HBM), after)


def slabs_of(refs, count, width):
    ny = refs[0].shape[1]
    for s in range(0, count, 2):
        pair = range(s, min(s + 2, count))
        columns = [jnp.concatenate([ref[q * width : (q + 1) * width] for ref in refs], axis=0) for q in pair]
        yield s * ny, (s + len(columns)) * ny, halves(jnp.concatenate(columns, axis=1))


def rest_of(refs, count, left, width):
    blocks = [ref[count * width :] for ref in refs]
    slabs = [[block[:, k * width : (k + 1) * width] for block in blocks] for k in range(left)]
    return halves(jnp.concatenate([jnp.concatenate(parts, axis=1) for parts in slabs], axis=0))


def widen(value, lanes):
    return jnp.concatenate([value, jnp.zeros((value.shape[0], lanes - value.shape[1]), F32)], axis=1)


def project_kernel(count, left, width, me_ref, start_ref, *refs):
    chips, me = (start_ref.shape[1] // width) // 2, me_ref[0]
    refs, (out_ref, high_ref, low_ref, *rest_refs) = refs[:chips][::-1], refs[chips:]
    ny = refs[0].shape[1]
    parts = [start_ref[:, i * width : (i + 1) * width] for i in range(2 * chips)]
    odd = (me & 1) != 0
    start = jnp.where(odd, jnp.concatenate(parts[1::2], axis=1), jnp.concatenate(parts[::2], axis=1))
    start = stack(reorder(start, lax.div(me, 2), chips, 1))
    for at, to, slab in slabs_of(refs, count, width):
        out_ref[:, at:to] = dot_split(start, slab, NN)
        high_ref[at // (2 * ny), :, : to - at], low_ref[at // (2 * ny), :, : to - at] = slab
    if left:
        rest = rest_of(refs, count, left, width)
        rest_refs[0][...], rest_refs[1][...] = rest
        out_ref[:, count * ny :] = widen(dot_split(start, rest, NT), ny)


def project(blocks, start_t, me, count, left, width):
    chips, ny = len(blocks), blocks[0].shape[1]
    pairs = jax.ShapeDtypeStruct(((count + 1) // 2, chips * width, 2 * ny), BF16)
    rest = [jax.ShapeDtypeStruct((left * (ny // chips), chips * width), BF16)] * 2 if left else []
    columns = jax.ShapeDtypeStruct((start_t.shape[0], (count + (left > 0)) * ny), F32)
    return pl.pallas_call(
        functools.partial(project_kernel, count, left, width),
        in_specs=[SMEM] + [VMEM] * (1 + chips),
        out_specs=[VMEM] * (3 + len(rest)),
        out_shape=[columns, pairs, pairs] + rest,
        compiler_params=PARAMS,
    )(me, start_t, *reversed(blocks))


def split_slabs(high_ref, low_ref, count, ny):
    for s in range(0, count, 2):
        to = min(s + 2, count)
        lanes = slice(0, (to - s) * ny)
        yield s * ny, to * ny, (high_ref[s // 2, :, lanes], low_ref[s // 2, :, lanes])


def raw_kernel(count, ny, chips, more, rest, last, me_ref, mine_ref, other_ref, high_ref, low_ref, *refs):
    refs, out_ref = refs[:-1], refs[-1]
    total = refs[0][...] if more else jnp.zeros(out_ref.shape, F32)
    for at, to, slab in split_slabs(high_ref, low_ref, count, ny):
        total += dot_split(stack(mine_ref[:, at:to] + other_ref[:, at:to]), slab, NT)
    if rest:
        halves_of_rest = (refs[-2][...], refs[-1][...])
        lanes = slice(count * ny, count * ny + halves_of_rest[0].shape[0])
        total += dot_split(stack(mine_ref[:, lanes] + other_ref[:, lanes]), halves_of_rest, NN)
    if last:
        total = reorder(total, lax.div(me_ref[0], 2), chips, 1)
    out_ref[...] = total


def raw_part(mine, other, split, before, me, count, ny, chips, last):
    pairs, rest = split[:2], split[2:]
    more = [] if before is None else [before]
    args = [me, mine, other, *pairs, *more, *rest]
    return pl.pallas_call(
        functools.partial(raw_kernel, count, ny, chips, bool(more), bool(rest), last),
        in_specs=[SMEM] + [VMEM] * (len(args) - 1),
        out_specs=VMEM,
        out_shape=jax.ShapeDtypeStruct((mine.shape[0], pairs[0].shape[1]), F32),
        compiler_params=PARAMS,
    )(*args)


def sum_over(value, axis, low, size):
    while low < size:
        masks = [low] if 2 * low >= size else [low, 2 * low, 3 * low]
        got = [exchange(value, axis, mask, size) for mask in far_first(masks)]
        for term in reversed(got):
            value = value + term
        low *= len(masks) + 1
    return value


def sum_round(value, axis, size):
    ring, low = [0, 1, 3, 2], 1
    while low < size:
        if 2 * low == size:
            return value + exchange(value, axis, low, size)
        got = []
        for step in range(1, 4):
            digits = [(i // low) % 4 for i in range(size)]
            to = [ring[(ring.index(digit) + step) % 4] for digit in digits]
            pairs = [(i, i + (to[i] - digits[i]) * low) for i in range(size)]
            got.append(lax.ppermute(value, axis, pairs))
        for term in reversed(got):
            value = value + term
        low *= 4
    return value


def gram_kernel(raw_ref, out_ref):
    raw = raw_ref[...]
    out_ref[...] = lax.dot_general(raw, raw, NT, precision=HIGHEST, preferred_element_type=F32)


def gram_part(raw):
    return pl.pallas_call(
        gram_kernel,
        in_specs=[VMEM],
        out_specs=VMEM,
        out_shape=jax.ShapeDtypeStruct((raw.shape[0], raw.shape[0]), F32),
        compiler_params=PARAMS,
    )(raw)


def inverse_factor(gram):
    rank = gram.shape[0]
    row = lax.broadcasted_iota(jnp.int32, (rank, rank), 0)
    col = lax.broadcasted_iota(jnp.int32, (rank, rank), 1)
    table = jnp.concatenate([gram, jnp.where(row == col, 1.0, 0.0).astype(F32)], axis=1)
    count = rank // 8
    rows = [table[8 * b : 8 * b + 8] for b in range(count)]
    wide = rows[0].shape
    sub = lax.broadcasted_iota(jnp.int32, wide, 0)

    def spread(value, k):
        return jnp.broadcast_to(value[k : k + 1], wide)

    def panel(i, b):
        return [jnp.broadcast_to(rows[i][:, 8 * b + k : 8 * b + k + 1], wide) for k in range(8)]

    inverse = []
    head = panel(0, 0)
    for b in range(count):
        below = {i: panel(i, b) for i in range(b + 1, count)}
        side, following = (panel(b, b + 1), panel(b + 1, b + 1)) if below else ([], [])
        pivots = jnp.ones(wide, F32)
        for k in range(8):
            pivot = spread(head[k], k)
            pivots = jnp.where(sub == k, pivot, pivots)
            scale = 1.0 / pivot
            factor = jnp.where(sub > k, head[k], 0.0)
            ahead = [spread(column, k) for column in head[k + 1 :]]
            head[k + 1 :] = [column - (factor * term) * scale for column, term in zip(head[k + 1 :], ahead)]
            factor = factor * scale
            across, beyond = spread(rows[b], k), [spread(column, k) for column in side]
            rows[b] = rows[b] - factor * across
            side = [column - factor * term for column, term in zip(side, beyond)]
            for i, columns in below.items():
                factor = columns[k] * scale
                columns[k + 1 :] = [column - factor * term for column, term in zip(columns[k + 1 :], ahead)]
                rows[i] = rows[i] - factor * across
                if i == b + 1:
                    following = [column - factor * term for column, term in zip(following, beyond)]
        inverse.append(rows[b][:, rank:] * lax.rsqrt(pivots[:, rank:]))
        head = following
    return jnp.concatenate(inverse, axis=0)


def factor_kernel(mine_ref, other_ref, out_ref):
    out_ref[...] = inverse_factor(mine_ref[...] + other_ref[...])


def factor(mine, other):
    return pl.pallas_call(
        factor_kernel,
        in_specs=[VMEM] * 2,
        out_specs=VMEM,
        out_shape=jax.ShapeDtypeStruct(mine.shape, F32),
        compiler_params=PARAMS,
        cost_estimate=pl.CostEstimate(flops=10**10, bytes_accessed=1000, transcendentals=0),
    )(mine, other)


def mixed_kernel(counts, chips, ny, after, me_ref, raw_ref, *refs):
    del after
    refs, out_ref = refs[:-1], refs[-1]
    raw = stack(reorder(raw_ref[...], lax.div(me_ref[0], 2), chips, 1))
    done = 0
    for c, count in enumerate(counts):
        for at, to, slab in split_slabs(refs[2 * c], refs[2 * c + 1], count, ny):
            out_ref[:, done + at : done + to] = dot_split(raw, slab, NN)
        done += count * ny
    out_ref[:, done:] = widen(dot_split(raw, (refs[-2][...], refs[-1][...]), NT), ny)


def mixed(raw, pairs, me, after, counts, chips, ny):
    return pl.pallas_call(
        functools.partial(mixed_kernel, counts, chips, ny),
        in_specs=[pl.BlockSpec(memory_space=pl.ANY), SMEM] + [VMEM] * (1 + len(pairs)),
        out_specs=VMEM,
        out_shape=jax.ShapeDtypeStruct((raw.shape[0], (sum(counts) + 1) * ny), F32),
        compiler_params=PARAMS,
    )(after, me, raw, *pairs)


def core_kernel(chips, me_ref, inverse_ref, mine_ref, other_ref, *outs):
    slabs, each, ny = outs[0].shape
    inverse = reorder(inverse_ref[...], me_ref[0], 2 * chips, 0)
    inverse = stack(jnp.concatenate([inverse[2 * k * each : (2 * k + 1) * each] for k in range(chips)], axis=0))
    for s in range(0, slabs, 2):
        to = min(s + 2, slabs)
        both = mine_ref[:, s * ny : to * ny] + other_ref[:, s * ny : to * ny]
        value = dot_split(inverse, halves(both), NN)
        for k in range(chips):
            for slab in range(s, to):
                lanes = slice((slab - s) * ny, (slab - s + 1) * ny)
                outs[k][slab] = value[k * each : (k + 1) * each, lanes]


def core(inverse, mine, other, me, chips, each, ny):
    return pl.pallas_call(
        functools.partial(core_kernel, chips),
        in_specs=[SMEM] + [VMEM] * 3,
        out_specs=[VMEM] * chips,
        out_shape=[jax.ShapeDtypeStruct((mine.shape[1] // ny, each, ny), F32)] * chips,
        compiler_params=PARAMS,
    )(me, inverse, mine, other)


def place_kernel(own, left, cells, me_ref, *refs):
    refs, (out_ref, rest, sems) = refs[:-3], refs[-3:]
    chips = len(refs)
    refs = in_order(refs)
    chip = lax.div(me_ref[0], 2)
    copies = []
    for k, ref in enumerate(refs):
        to = out_ref.at[pl.ds((chip ^ k) * own, own)]
        copies.append(pltpu.make_async_copy(ref.at[pl.ds(0, own)], to, sems.at[k]))
        copies[-1].start()
    for k in range(left):
        parts = [ref[own][:, k * cells : (k + 1) * cells] for ref in refs]
        rest[k] = reorder(jnp.concatenate(parts, axis=1), chip, chips, 1)
    copies.append(pltpu.make_async_copy(rest, out_ref.at[pl.ds(chips * own, left)], sems.at[chips]))
    copies[-1].start()
    for copy in copies:
        copy.wait()


def place(parts, me, own, left):
    chips = len(parts)
    _, each, ny = parts[0].shape
    return pl.pallas_call(
        functools.partial(place_kernel, own, left, ny // chips),
        in_specs=[SMEM] + [VMEM] * chips,
        out_specs=HBM,
        out_shape=jax.ShapeDtypeStruct((chips * own + left, each, ny), F32),
        scratch_shapes=[pltpu.VMEM((left, each, ny), F32), pltpu.SemaphoreType.DMA((chips + 1,))],
        compiler_params=PARAMS,
    )(me, *for_order(parts))


def shards(n, layers, field_data, start_block):
    species, planes, width, ny = field_data.shape
    chips, each = n // 2, start_block.shape[1] // n
    total = species * planes
    own, left = divmod(total, chips)
    counts = [own * 3 // 8, own * 3 // 8]
    counts.append(own - sum(counts))
    me = lax.axis_index("fib").astype(jnp.int32).reshape(1)
    rows = field_data.reshape(total * width, ny)
    start_t = start_block.T
    bounds, first = [], 0
    for c, count in enumerate(counts):
        bounds.append((first, first + count, left if c == 1 else 0))
        first += count
    near, far = [*range(1, chips - 1)], [chips - 1]
    sent, after = [{} for _ in counts], me
    for c, ks in [(0, far), (0, [0, *near]), (1, [0, *near, *far]), (2, [0, *near, *far])]:
        got = pack(rows, me, after, ks, chips, *bounds[c][:2], own, bounds[c][2], width)
        sent[c].update(zip(ks, got))
        after = got[0]
    pairs, rests, raw = [], [], None
    for c, (first, last, rest) in enumerate(bounds):
        part = [sent[c][0]] + [exchange(sent[c][k], "fib", 2 * k, n) for k in range(1, chips)]
        mine, *split = project(part, start_t, me, last - first, rest, width)
        other = exchange(mine, "fib", 1, n)
        raw = raw_part(mine, other, split, raw, me, last - first, ny, chips, last == own)
        pairs += split[:2]
        rests += split[2:]
    raw = sum_round(sum_over(raw, "fib", 2, n), "blk", layers)
    gram = gram_part(raw)
    sums = mixed(raw, pairs + rests, me, gram, counts, chips, ny)
    inverse = factor(gram, exchange(gram, "fib", 1, n))
    parts = core(inverse, sums, exchange(sums, "fib", 1, n), me, chips, each, ny)
    parts = [parts[0]] + [exchange(parts[k], "fib", 2 * k, n) for k in range(1, chips)]
    return place(parts, me, own, left).reshape(species, planes, each, ny)


def solution(mesh):
    n, layers = mesh.shape["fib"], mesh.shape["blk"]
    in_specs = (P(None, "blk", "fib", None), P())
    out_specs = P(None, "blk", "fib", None)
    return jax.shard_map(
        functools.partial(shards, n, layers), mesh=mesh, in_specs=in_specs, out_specs=out_specs, check_vma=False
    )
```

```python
import functools

import jax
import jax.numpy as jnp
from jax import lax
from jax.experimental import pallas as pl
from jax.experimental.pallas import tpu as pltpu
from jax.sharding import PartitionSpec as P

F32, BF16 = jnp.float32, jnp.bfloat16
HIGHEST = lax.Precision.HIGHEST
NN = (((1,), (0,)), ((), ()))
NT = (((1,), (1,)), ((), ()))
PARAMS = pltpu.CompilerParams(vmem_limit_bytes=40 * 1024 * 1024)
VMEM = pl.BlockSpec(memory_space=pltpu.VMEM)
SMEM = pl.BlockSpec(memory_space=pltpu.SMEM)
HBM = pl.BlockSpec(memory_space=pltpu.HBM)


def halves(value):
    high = value.astype(BF16)
    return high, (value - high.astype(F32)).astype(BF16)


def stack(value):
    return jnp.concatenate(halves(value), axis=0)


def dot(left, right, dims):
    return lax.dot_general(left, right, dims, preferred_element_type=F32)


def dot_split(left, right, dims):
    rows = left.shape[0] // 2
    right_high, right_low = right
    both = dot(left, right_high, dims)
    return both[:rows] + both[rows:] + dot(left[:rows], right_low, dims)


def reorder(value, me, n, axis):
    width = value.shape[axis] // n
    bit = 1
    while bit < n:
        parts = [lax.slice_in_dim(value, i * bit * width, (i + 1) * bit * width, axis=axis) for i in range(n // bit)]
        swapped = jnp.concatenate([parts[i ^ 1] for i in range(n // bit)], axis=axis)
        value = jnp.where((me & bit) != 0, swapped, value)
        bit *= 2
    return value


def far_first(masks):
    return [masks[-1], *masks[:-1]]


def for_order(blocks):
    return [blocks[k] for k in [*far_first(range(1, len(blocks))), 0]]


def in_order(refs):
    return [refs[-1], *refs[1:-1], refs[0]]


def exchange(value, axis, mask, size):
    return lax.ppermute(value, axis, [(i, i ^ mask) for i in range(size)])


def pack_kernel(ks, chips, first, last, own, left, width, me_ref, rows_ref, after, *refs):
    del after
    blocks, refs = refs[: len(ks)], refs[len(ks) :]
    ny = rows_ref.shape[1]
    chip = lax.div(me_ref[0], 2)
    sems = refs[-1]
    count = (last - first) * width
    if left:
        turned, rest = refs[:2]
        rest_copy = pltpu.make_async_copy(rows_ref.at[pl.ds(chips * own * width, left * width)], rest, sems.at[chips])
        rest_copy.start()
    copies = []
    for k, block in zip(ks, blocks):
        at = pl.multiple_of(((chip ^ k) * own + first) * width, 8)
        copies.append(pltpu.make_async_copy(rows_ref.at[pl.ds(at, count)], block.at[pl.ds(0, count)], sems.at[k]))
        copies[-1].start()
    if left:
        cells = ny // chips
        rest_copy.wait()
        turned[:, : left * width] = rest[...].T
        for k, block in zip(ks, blocks):
            block[count:] = turned[pl.ds(pl.multiple_of((chip ^ k) * cells, cells), cells), :]
    for copy in copies:
        copy.wait()


def pack(rows, me, after, ks, chips, first, last, own, left, width):
    ny = rows.shape[1]
    high = (last - first) * width + (ny // chips if left else 0)
    scratch = [pltpu.VMEM((ny, ny), F32), pltpu.VMEM((left * width, ny), F32)] if left else []
    return pl.pallas_call(
        functools.partial(pack_kernel, ks, chips, first, last, own, left, width),
        in_specs=[SMEM, HBM, pl.BlockSpec(memory_space=pl.ANY)],
        out_specs=[VMEM] * len(ks),
        out_shape=[jax.ShapeDtypeStruct((high, ny), F32)] * len(ks),
        scratch_shapes=scratch + [pltpu.SemaphoreType.DMA((chips + 1,))],
        compiler_params=PARAMS,
    )(me, pltpu.with_memory_space_constraint(rows, pltpu.HBM), after)


def slabs_of(refs, count, width):
    ny = refs[0].shape[1]
    for s in range(0, count, 2):
        pair = range(s, min(s + 2, count))
        columns = [jnp.concatenate([ref[q * width : (q + 1) * width] for ref in refs], axis=0) for q in pair]
        yield s * ny, (s + len(columns)) * ny, halves(jnp.concatenate(columns, axis=1))


def rest_of(refs, count, left, width):
    blocks = [ref[count * width :] for ref in refs]
    slabs = [[block[:, k * width : (k + 1) * width] for block in blocks] for k in range(left)]
    return halves(jnp.concatenate([jnp.concatenate(parts, axis=1) for parts in slabs], axis=0))


def widen(value, lanes):
    return jnp.concatenate([value, jnp.zeros((value.shape[0], lanes - value.shape[1]), F32)], axis=1)


def project_kernel(count, left, width, me_ref, start_ref, *refs):
    chips, me = (start_ref.shape[1] // width) // 2, me_ref[0]
    refs, (out_ref, high_ref, low_ref, *rest_refs) = refs[:chips][::-1], refs[chips:]
    ny = refs[0].shape[1]
    parts = [start_ref[:, i * width : (i + 1) * width] for i in range(2 * chips)]
    odd = (me & 1) != 0
    start = jnp.where(odd, jnp.concatenate(parts[1::2], axis=1), jnp.concatenate(parts[::2], axis=1))
    start = stack(reorder(start, lax.div(me, 2), chips, 1))
    for at, to, slab in slabs_of(refs, count, width):
        out_ref[:, at:to] = dot_split(start, slab, NN)
        high_ref[at // (2 * ny), :, : to - at], low_ref[at // (2 * ny), :, : to - at] = slab
    if left:
        rest = rest_of(refs, count, left, width)
        rest_refs[0][...], rest_refs[1][...] = rest
        out_ref[:, count * ny :] = widen(dot_split(start, rest, NT), ny)


def project(blocks, start_t, me, count, left, width):
    chips, ny = len(blocks), blocks[0].shape[1]
    pairs = jax.ShapeDtypeStruct(((count + 1) // 2, chips * width, 2 * ny), BF16)
    rest = [jax.ShapeDtypeStruct((left * (ny // chips), chips * width), BF16)] * 2 if left else []
    columns = jax.ShapeDtypeStruct((start_t.shape[0], (count + (left > 0)) * ny), F32)
    return pl.pallas_call(
        functools.partial(project_kernel, count, left, width),
        in_specs=[SMEM] + [VMEM] * (1 + chips),
        out_specs=[VMEM] * (3 + len(rest)),
        out_shape=[columns, pairs, pairs] + rest,
        compiler_params=PARAMS,
    )(me, start_t, *reversed(blocks))


def split_slabs(high_ref, low_ref, count, ny):
    for s in range(0, count, 2):
        to = min(s + 2, count)
        lanes = slice(0, (to - s) * ny)
        yield s * ny, to * ny, (high_ref[s // 2, :, lanes], low_ref[s // 2, :, lanes])


def raw_kernel(count, ny, chips, more, rest, last, me_ref, mine_ref, other_ref, high_ref, low_ref, *refs):
    refs, out_ref = refs[:-1], refs[-1]
    total = refs[0][...] if more else jnp.zeros(out_ref.shape, F32)
    for at, to, slab in split_slabs(high_ref, low_ref, count, ny):
        total += dot_split(stack(mine_ref[:, at:to] + other_ref[:, at:to]), slab, NT)
    if rest:
        halves_of_rest = (refs[-2][...], refs[-1][...])
        lanes = slice(count * ny, count * ny + halves_of_rest[0].shape[0])
        total += dot_split(stack(mine_ref[:, lanes] + other_ref[:, lanes]), halves_of_rest, NN)
    if last:
        total = reorder(total, lax.div(me_ref[0], 2), chips, 1)
    out_ref[...] = total


def raw_part(mine, other, split, before, me, count, ny, chips, last):
    pairs, rest = split[:2], split[2:]
    more = [] if before is None else [before]
    args = [me, mine, other, *pairs, *more, *rest]
    return pl.pallas_call(
        functools.partial(raw_kernel, count, ny, chips, bool(more), bool(rest), last),
        in_specs=[SMEM] + [VMEM] * (len(args) - 1),
        out_specs=VMEM,
        out_shape=jax.ShapeDtypeStruct((mine.shape[0], pairs[0].shape[1]), F32),
        compiler_params=PARAMS,
    )(*args)


def sum_over(value, axis, low, size):
    while low < size:
        masks = [low] if 2 * low >= size else [low, 2 * low, 3 * low]
        got = [exchange(value, axis, mask, size) for mask in far_first(masks)]
        for term in reversed(got):
            value = value + term
        low *= len(masks) + 1
    return value


def sum_round(value, axis, size):
    ring, low = [0, 1, 3, 2], 1
    while low < size:
        if 2 * low == size:
            return value + exchange(value, axis, low, size)
        got = []
        for step in range(1, 4):
            digits = [(i // low) % 4 for i in range(size)]
            to = [ring[(ring.index(digit) + step) % 4] for digit in digits]
            pairs = [(i, i + (to[i] - digits[i]) * low) for i in range(size)]
            got.append(lax.ppermute(value, axis, pairs))
        for term in reversed(got):
            value = value + term
        low *= 4
    return value


def gram_kernel(raw_ref, out_ref):
    raw = raw_ref[...]
    out_ref[...] = lax.dot_general(raw, raw, NT, precision=HIGHEST, preferred_element_type=F32)


def gram_part(raw):
    return pl.pallas_call(
        gram_kernel,
        in_specs=[VMEM],
        out_specs=VMEM,
        out_shape=jax.ShapeDtypeStruct((raw.shape[0], raw.shape[0]), F32),
        compiler_params=PARAMS,
    )(raw)


def inverse_factor(gram):
    rank = gram.shape[0]
    row = lax.broadcasted_iota(jnp.int32, (rank, rank), 0)
    col = lax.broadcasted_iota(jnp.int32, (rank, rank), 1)
    table = jnp.concatenate([gram, jnp.where(row == col, 1.0, 0.0).astype(F32)], axis=1)
    count = rank // 8
    rows = [table[8 * b : 8 * b + 8] for b in range(count)]
    wide = rows[0].shape
    sub = lax.broadcasted_iota(jnp.int32, wide, 0)

    def spread(value, k):
        return jnp.broadcast_to(value[k : k + 1], wide)

    def panel(i, b):
        return [jnp.broadcast_to(rows[i][:, 8 * b + k : 8 * b + k + 1], wide) for k in range(8)]

    inverse = []
    head = panel(0, 0)
    for b in range(count):
        below = {i: panel(i, b) for i in range(b + 1, count)}
        side, following = (panel(b, b + 1), panel(b + 1, b + 1)) if below else ([], [])
        pivots = jnp.ones(wide, F32)
        for k in range(8):
            pivot = spread(head[k], k)
            pivots = jnp.where(sub == k, pivot, pivots)
            scale = 1.0 / pivot
            factor = jnp.where(sub > k, head[k], 0.0)
            ahead = [spread(column, k) for column in head[k + 1 :]]
            head[k + 1 :] = [column - (factor * term) * scale for column, term in zip(head[k + 1 :], ahead)]
            factor = factor * scale
            across, beyond = spread(rows[b], k), [spread(column, k) for column in side]
            rows[b] = rows[b] - factor * across
            side = [column - factor * term for column, term in zip(side, beyond)]
            for i, columns in below.items():
                factor = columns[k] * scale
                columns[k + 1 :] = [column - factor * term for column, term in zip(columns[k + 1 :], ahead)]
                rows[i] = rows[i] - factor * across
                if i == b + 1:
                    following = [column - factor * term for column, term in zip(following, beyond)]
        inverse.append(rows[b][:, rank:] * lax.rsqrt(pivots[:, rank:]))
        head = following
    return jnp.concatenate(inverse, axis=0)


def factor_kernel(mine_ref, other_ref, out_ref):
    out_ref[...] = inverse_factor(mine_ref[...] + other_ref[...])


def factor(mine, other):
    return pl.pallas_call(
        factor_kernel,
        in_specs=[VMEM] * 2,
        out_specs=VMEM,
        out_shape=jax.ShapeDtypeStruct(mine.shape, F32),
        compiler_params=PARAMS,
        cost_estimate=pl.CostEstimate(flops=10**10, bytes_accessed=1000, transcendentals=0),
    )(mine, other)


def mixed_kernel(counts, chips, ny, after, me_ref, raw_ref, *refs):
    del after
    refs, out_ref = refs[:-1], refs[-1]
    raw = stack(reorder(raw_ref[...], lax.div(me_ref[0], 2), chips, 1))
    done = 0
    for c, count in enumerate(counts):
        for at, to, slab in split_slabs(refs[2 * c], refs[2 * c + 1], count, ny):
            out_ref[:, done + at : done + to] = dot_split(raw, slab, NN)
        done += count * ny
    out_ref[:, done:] = widen(dot_split(raw, (refs[-2][...], refs[-1][...]), NT), ny)


def mixed(raw, pairs, me, after, counts, chips, ny):
    return pl.pallas_call(
        functools.partial(mixed_kernel, counts, chips, ny),
        in_specs=[pl.BlockSpec(memory_space=pl.ANY), SMEM] + [VMEM] * (1 + len(pairs)),
        out_specs=VMEM,
        out_shape=jax.ShapeDtypeStruct((raw.shape[0], (sum(counts) + 1) * ny), F32),
        compiler_params=PARAMS,
    )(after, me, raw, *pairs)


def core_kernel(chips, me_ref, inverse_ref, mine_ref, other_ref, *outs):
    slabs, each, ny = outs[0].shape
    inverse = reorder(inverse_ref[...], me_ref[0], 2 * chips, 0)
    inverse = stack(jnp.concatenate([inverse[2 * k * each : (2 * k + 1) * each] for k in range(chips)], axis=0))
    for s in range(0, slabs, 2):
        to = min(s + 2, slabs)
        both = mine_ref[:, s * ny : to * ny] + other_ref[:, s * ny : to * ny]
        value = dot_split(inverse, halves(both), NN)
        for k in range(chips):
            for slab in range(s, to):
                lanes = slice((slab - s) * ny, (slab - s + 1) * ny)
                outs[k][slab] = value[k * each : (k + 1) * each, lanes]


def core(inverse, mine, other, me, chips, each, ny):
    return pl.pallas_call(
        functools.partial(core_kernel, chips),
        in_specs=[SMEM] + [VMEM] * 3,
        out_specs=[VMEM] * chips,
        out_shape=[jax.ShapeDtypeStruct((mine.shape[1] // ny, each, ny), F32)] * chips,
        compiler_params=PARAMS,
    )(me, inverse, mine, other)


def place_kernel(own, left, cells, me_ref, *refs):
    refs, (out_ref, rest, sems) = refs[:-3], refs[-3:]
    chips = len(refs)
    refs = in_order(refs)
    chip = lax.div(me_ref[0], 2)
    for k in range(left):
        parts = [ref[own][:, k * cells : (k + 1) * cells] for ref in refs]
        rest[k] = reorder(jnp.concatenate(parts, axis=1), chip, chips, 1)
    copies = []
    for k, ref in enumerate(refs):
        to = out_ref.at[pl.ds((chip ^ k) * own, own)]
        copies.append(pltpu.make_async_copy(ref.at[pl.ds(0, own)], to, sems.at[k]))
        copies[-1].start()
    copies.append(pltpu.make_async_copy(rest, out_ref.at[pl.ds(chips * own, left)], sems.at[chips]))
    copies[-1].start()
    for copy in copies:
        copy.wait()


def place(parts, me, own, left):
    chips = len(parts)
    _, each, ny = parts[0].shape
    return pl.pallas_call(
        functools.partial(place_kernel, own, left, ny // chips),
        in_specs=[SMEM] + [VMEM] * chips,
        out_specs=HBM,
        out_shape=jax.ShapeDtypeStruct((chips * own + left, each, ny), F32),
        scratch_shapes=[pltpu.VMEM((left, each, ny), F32), pltpu.SemaphoreType.DMA((chips + 1,))],
        compiler_params=PARAMS,
    )(me, *for_order(parts))


def shards(n, layers, field_data, start_block):
    species, planes, width, ny = field_data.shape
    chips, each = n // 2, start_block.shape[1] // n
    total = species * planes
    own, left = divmod(total, chips)
    counts = [own * 3 // 8, own * 3 // 8]
    counts.append(own - sum(counts))
    me = lax.axis_index("fib").astype(jnp.int32).reshape(1)
    rows = field_data.reshape(total * width, ny)
    start_t = start_block.T
    bounds, first = [], 0
    for c, count in enumerate(counts):
        bounds.append((first, first + count, left if c == 1 else 0))
        first += count
    near, far = [*range(1, chips - 1)], [chips - 1]
    sent, after = [{} for _ in counts], me
    for c, ks in [(0, far), (0, [0, *near]), (1, [0, *near, *far]), (2, [0, *near, *far])]:
        got = pack(rows, me, after, ks, chips, *bounds[c][:2], own, bounds[c][2], width)
        sent[c].update(zip(ks, got))
        after = got[0]
    pairs, rests, raw = [], [], None
    for c, (first, last, rest) in enumerate(bounds):
        part = [sent[c][0]] + [exchange(sent[c][k], "fib", 2 * k, n) for k in range(1, chips)]
        mine, *split = project(part, start_t, me, last - first, rest, width)
        other = exchange(mine, "fib", 1, n)
        raw = raw_part(mine, other, split, raw, me, last - first, ny, chips, last == own)
        pairs += split[:2]
        rests += split[2:]
    raw = sum_round(sum_over(raw, "fib", 2, n), "blk", layers)
    gram = gram_part(raw)
    sums = mixed(raw, pairs + rests, me, gram, counts, chips, ny)
    inverse = factor(gram, exchange(gram, "fib", 1, n))
    parts = core(inverse, sums, exchange(sums, "fib", 1, n), me, chips, each, ny)
    parts = [parts[0]] + [exchange(parts[k], "fib", 2 * k, n) for k in range(1, chips)]
    return place(parts, me, own, left).reshape(species, planes, each, ny)


def solution(mesh):
    n, layers = mesh.shape["fib"], mesh.shape["blk"]
    in_specs = (P(None, "blk", "fib", None), P())
    out_specs = P(None, "blk", "fib", None)
    return jax.shard_map(
        functools.partial(shards, n, layers), mesh=mesh, in_specs=in_specs, out_specs=out_specs, check_vma=False
    )
```
